256 devices in a mesh: dp: 16 (over x_lo, z), space: 16 (over y, x_hi, core).
Axes of the slice: x: 4 (x_hi: 2, x_lo: 2; x = x_hi * 2 + x_lo), y: 4, z: 8, core: 2. Of those that a mesh axis runs over, the one named last changes fastest.
Arguments:
- volume: bfloat16 [16, 32, 32, 8, 256], P('dp', None, 'space'), may hold values from -6 to 6
- conv_weight: bfloat16 [64, 864], replicated, may hold values from -0.21875 to 0.21875
- strided_weight: bfloat16 [128, 512], P('space'), may hold values from -0.25 to 0.25
- cotangent: bfloat16 [16, 128, 16, 4, 128], P('dp', 'space'), may hold values from -6 to 6
Outputs:
- output: bfloat16 [16, 128, 16, 4, 128], P('dp', 'space')
- vol_grad: bfloat16 [16, 32, 32, 8, 256], P('dp', None, 'space')
- conv_grad: float32 [64, 864], replicated
- strided_grad: float32 [128, 512], P('space')
The draws below stay inside these ranges and needn't reach their ends.
All inputs are finite; a program needn't handle non-finite values.
Results may differ from the reference program's by a relative error of at most 0.0095.
Values may be sent and summed in bfloat16 or wider, within the bound.
No kernel may reach another device: no remote copies, remote signals or barrier semaphores. Data moves between devices by JAX's collectives and lax.ppermute only.
A program may use at most 128 MiB of HBM per device.

```python
import math
import jax
import jax.numpy as jnp
from jax import lax

CI = 32
CM = 64
CO = 128
ROWS = 8
COLS = 256
SAMPLES = 16
Z = 32


def block_scale(own_key, shape, split, low, largest):
    level, own = 1.0, jax.random.fold_in(own_key, 6)
    for dim, blocks in split:
        heights = jnp.exp(jax.random.uniform(jax.random.fold_in(own, dim), (blocks,), jnp.float32, low / len(split), largest / len(split)))
        level = level * jnp.repeat(heights, shape[dim] // blocks).reshape([-1 if axis == dim else 1 for axis in range(len(shape))])
    return level


def bell_draw(key, shape, spread, reach, cuts=(), held_as=jnp.bfloat16):
    result = spread * jax.random.normal(key, shape, jnp.float32)
    if cuts:
        result = result * block_scale(key, shape, cuts, -0.22, 0.18)
    return jnp.clip(result, -reach, reach).astype(held_as)


def setup_inputs(seed: int = 0) -> dict:
    streams_of = jax.random.split(jax.random.key(seed), 5)
    volume = bell_draw(streams_of[0], (SAMPLES, CI, Z, ROWS, COLS), 1.0, 6.0, ((0, 16), (2, 16)))
    conv_weight = bell_draw(streams_of[1], (CM, 27 * CI), (27 * CI) ** -0.5, 0.21875)
    strided_weight = bell_draw(streams_of[2], (CO, 8 * CM), (8 * CM) ** -0.5, 0.25, ((0, 16),))
    cotangent = bell_draw(streams_of[3], (SAMPLES, CO, Z // 2, ROWS // 2, COLS // 2), 1.0, 6.0, ((0, 16), (1, 16)))
    return {"volume": volume, "conv_weight": conv_weight, "strided_weight": strided_weight, "cotangent": cotangent}


root_two_pi = 0.7978845608028654

def gelu_value(field):
    inner = root_two_pi * (field + 0.044715 * field * field * field)
    return 0.5 * field * (1.0 + jnp.tanh(inner))

def gelu_slope(field):
    inner = root_two_pi * (field + 0.044715 * field * field * field)
    hyper = jnp.tanh(inner)
    return 0.5 * (1.0 + hyper) + 0.5 * field * (1.0 - hyper * hyper) * root_two_pi * (1.0 + 3.0 * 0.044715 * field * field)

def tap_stack(padded):
    depth_len = padded.shape[2] - 2
    row_count, col_count = (padded.shape[3], padded.shape[4])
    framed = jnp.pad(padded, ((0, 0), (0, 0), (0, 0), (1, 1), (1, 1)))
    pieces = [framed[:, :, a:a + depth_len, b:b + row_count, e:e + col_count] for a in range(3) for b in range(3) for e in range(3)]
    return jnp.concatenate(pieces, axis=1)

def to_blocks(field):
    samples, channels = (field.shape[0], field.shape[1])
    row_count, col_count = (field.shape[-2], field.shape[-1])
    pairs = field.size // (samples * channels * row_count * col_count * 2)
    shaped = field.reshape(samples, channels, pairs, 2, row_count // 2, 2, col_count // 2, 2)
    return shaped.transpose(0, 3, 5, 7, 1, 2, 4, 6).reshape(samples, 8 * channels, pairs, row_count // 2, col_count // 2)

def from_blocks(blocked):
    samples, widened, pairs, half_rows, half_cols = blocked.shape
    channels = widened // 8
    shaped = blocked.reshape(samples, 2, 2, 2, channels, pairs, half_rows, half_cols)
    return shaped.transpose(0, 4, 5, 1, 6, 2, 7, 3).reshape(samples, channels, 2 * pairs, 2 * half_rows, 2 * half_cols)

def depth_pad(field):
    return jnp.pad(field, ((0, 0), (0, 0), (1, 1), (0, 0), (0, 0)))

def reference(volume, conv_weight, strided_weight, cotangent):
    mid_channels = conv_weight.shape[0]
    in_channels = volume.shape[1]
    conv_wide = conv_weight.astype(jnp.float32)
    strided_wide = strided_weight.astype(jnp.float32)
    flipped = conv_weight.reshape(mid_channels, 27, in_channels)[:, ::-1, :].transpose(2, 1, 0).reshape(in_channels, 27 * mid_channels).astype(jnp.float32)

    def one_sample(pair):
        sample_vol, sample_cot = pair
        vol_taps = tap_stack(depth_pad(sample_vol[None]))
        taps_wide = vol_taps.astype(jnp.float32)
        pre = jnp.einsum('ok,skdrw->sodrw', conv_wide, taps_wide)
        hidden = gelu_value(pre).astype(jnp.bfloat16)
        blocks = to_blocks(hidden).astype(jnp.float32)
        output = jnp.einsum('ok,skdrw->sodrw', strided_wide, blocks).astype(jnp.bfloat16)
        cot_wide = sample_cot[None].astype(jnp.float32)
        strided_part = jnp.einsum('sodrw,skdrw->ok', cot_wide, blocks)
        hidden_grad = from_blocks(jnp.einsum('ok,sodrw->skdrw', strided_wide, cot_wide))
        pre_grad = (hidden_grad * gelu_slope(pre)).astype(jnp.bfloat16)
        conv_part = jnp.einsum('sodrw,skdrw->ok', pre_grad.astype(jnp.float32), taps_wide)
        grad_taps = tap_stack(depth_pad(pre_grad)).astype(jnp.float32)
        vol_grad = jnp.einsum('ck,skdrw->scdrw', flipped, grad_taps).astype(jnp.bfloat16)
        return (output[0], vol_grad[0], conv_part, strided_part)
    output, vol_grad, conv_parts, strided_parts = lax.map(one_sample, (volume, cotangent))
    cells_total = volume.shape[0] * volume.shape[2] * volume.shape[3] * volume.shape[4]
    conv_grad = lax.optimization_barrier(jnp.sum(conv_parts, axis=0)) / math.sqrt(cells_total)
    strided_grad = lax.optimization_barrier(jnp.sum(strided_parts, axis=0)) / math.sqrt(cells_total / 8)
    return (output, vol_grad, conv_grad, strided_grad)
```

```python
import math

import jax
import jax.numpy as jnp
from jax import lax
from jax.sharding import PartitionSpec as P

root_two_pi = 0.7978845608028654
bf16 = jnp.bfloat16
f32 = jnp.float32


def column_split(cols):
    source = lax.broadcasted_iota(jnp.int32, (cols, cols), 0)
    place = lax.broadcasted_iota(jnp.int32, (cols, cols), 1)
    half = cols // 2
    return (source == 2 * (place % half) + place // half).astype(bf16)


def swap(parts, axis):
    return lax.all_to_all(parts, axis, 0, 0, tiled=True)


def neighbours(first, last, axis):
    count = lax.axis_size(axis)
    ends = count - 1
    before = lax.ppermute(last, axis, [(i, i + 1) for i in range(ends)])
    after = lax.ppermute(first, axis, [(i + 1, i) for i in range(ends)])
    return before, after


def column_variants(planes):
    even, odd = planes[:, :, 0], planes[:, :, 1]
    zero = jnp.zeros_like(even[..., :1])
    odd_before = jnp.concatenate([zero, odd[..., :-1]], axis=-1)
    even_after = jnp.concatenate([even[..., 1:], zero], axis=-1)
    return jnp.stack([odd_before, even, odd, even_after], axis=2)


def taps(planes):
    depth, rows = planes.shape[0] - 2, planes.shape[1]
    framed = jnp.pad(column_variants(planes), ((0, 0), (1, 1), (0, 0), (0, 0), (0, 0)))
    pieces = [framed[a : a + depth, b : b + rows] for a in range(3) for b in range(3)]
    stacked = jnp.stack(pieces, axis=0)
    ab, z, r, v, c, w = stacked.shape
    return stacked.transpose(0, 3, 4, 1, 2, 5).reshape(ab * v * c, z * r * w)


def shards(volume, conv_weight, strided_weight, cotangent):
    _, in_ch, depth, rows, cols = volume.shape
    mid = conv_weight.shape[0]
    own_out, wide = strided_weight.shape
    n_space, n_dp = lax.axis_size("space"), lax.axis_size("dp")
    half_rows, half = rows // 2, cols // 2
    cells = n_dp * depth * n_space * rows * cols
    split = column_split(cols)

    vol = jnp.einsum("czrx,xq->zrcq", volume[0], split, preferred_element_type=f32).astype(bf16)
    vol = vol.reshape(depth, rows, in_ch, 2, half).transpose(0, 1, 3, 2, 4)
    before, after = neighbours(vol[:1], vol[-1:], "space")
    cot = cotangent[0].transpose(1, 0, 2, 3).reshape(n_space, own_out, half_rows * half)
    both = jnp.concatenate([cot, jnp.broadcast_to(strided_weight[None], (n_space, own_out, wide))], axis=-1)
    both = swap(both, "space").reshape(n_space * own_out, -1)
    cot_slab, filters = both[:, : half_rows * half], both[:, half_rows * half :]

    vol_taps = taps(jnp.concatenate([before, vol, after], axis=0))
    weight = conv_weight.reshape(mid, 9, 3, in_ch)
    pad = jnp.zeros((mid, 9, 1, in_ch), bf16)
    weight_two = jnp.stack(
        [jnp.concatenate([weight, pad], axis=2), jnp.concatenate([pad, weight], axis=2)], axis=0
    ).reshape(2 * mid, 9 * 4 * in_ch)
    pre = jnp.dot(weight_two, vol_taps, preferred_element_type=f32)
    inner = root_two_pi * (pre + 0.044715 * pre * pre * pre)
    hyper = jnp.tanh(inner)
    hidden = (0.5 * pre * (1.0 + hyper)).astype(bf16)
    slope = 0.5 * (1.0 + hyper) + 0.5 * pre * (1.0 - hyper * hyper) * root_two_pi * (
        1.0 + 3.0 * 0.044715 * pre * pre
    )
    blocks = (
        hidden.reshape(2 * mid, depth, half_rows, 2, half).transpose(1, 3, 0, 2, 4).reshape(wide, half_rows * half)
    )
    hidden_grad = lax.dot_general(filters, cot_slab, (((0,), (0,)), ((), ())), preferred_element_type=f32)
    hidden_grad = (
        hidden_grad.reshape(depth, 2, 2 * mid, half_rows, half).transpose(2, 0, 3, 1, 4).reshape(2 * mid, -1)
    )
    pre_grad = (hidden_grad * slope).astype(bf16)
    grad_planes = pre_grad.reshape(2, mid, depth, rows, half).transpose(2, 3, 0, 1, 4)
    grad_before, grad_after = neighbours(grad_planes[:1], grad_planes[-1:], "space")

    out = jnp.dot(filters, blocks, preferred_element_type=f32).astype(bf16)
    strided_part = lax.dot_general(cot_slab, blocks, (((1,), (1,)), ((), ())), preferred_element_type=f32)
    conv_two = lax.dot_general(pre_grad, vol_taps, (((1,), (1,)), ((), ())), preferred_element_type=f32)
    conv_two = conv_two.reshape(2, mid, 9, 4, in_ch)
    conv_part = conv_two[0, :, :, :3] + conv_two[1, :, :, 1:]

    n_out = own_out * half_rows * half
    n_strided = own_out * wide
    mixed = jnp.concatenate(
        [
            out.reshape(n_space, n_out),
            strided_part.astype(bf16).reshape(n_space, n_strided),
            conv_part.astype(bf16).reshape(n_space, -1),
        ],
        axis=1,
    )
    mixed = swap(mixed.reshape(n_space, -1, 128), "space").reshape(n_space, -1)
    output = mixed[:, :n_out].reshape(1, n_space, own_out, half_rows, half).transpose(0, 2, 1, 3, 4)
    sums = jnp.sum(mixed[:, n_out:].astype(f32), axis=0).astype(bf16)
    sums = jnp.broadcast_to(sums.reshape(1, -1, 128), (n_dp, sums.size // 128, 128))
    sums = jnp.sum(swap(sums, "dp").astype(f32), axis=0).reshape(-1)
    strided_grad = sums[:n_strided].reshape(own_out, wide) / math.sqrt(cells / 8)
    conv_own = (sums[n_strided:] / math.sqrt(cells)).astype(bf16).reshape(1, -1, 128)
    conv_all = swap(jnp.broadcast_to(conv_own, (n_space,) + conv_own.shape[1:]), "space")
    conv_grad = conv_all.astype(f32).reshape(mid, 27 * in_ch)

    grad_taps = taps(jnp.concatenate([grad_before, grad_planes, grad_after], axis=0))
    back = weight.reshape(mid, 9, 3, in_ch)[:, ::-1, ::-1]
    back = jnp.stack(
        [jnp.concatenate([back, pad], axis=2), jnp.concatenate([pad, back], axis=2)], axis=0
    )
    back = back.transpose(0, 4, 2, 3, 1).reshape(2 * in_ch, 9 * 4 * mid)
    vol_grad = jnp.dot(back, grad_taps, preferred_element_type=f32).astype(bf16)
    vol_grad = vol_grad.reshape(2, in_ch, depth, rows, half).transpose(1, 2, 3, 0, 4).reshape(in_ch, depth, rows, cols)
    vol_grad = jnp.einsum("czrq,xq->czrx", vol_grad, split, preferred_element_type=f32).astype(bf16)[None]
    return output, vol_grad, conv_grad, strided_grad


def solution(mesh):
    return jax.shard_map(
        shards,
        mesh=mesh,
        in_specs=(
            P("dp", None, "space", None, None),
            P(),
            P("space", None),
            P("dp", "space", None, None, None),
        ),
        out_specs=(
            P("dp", "space", None, None, None),
            P("dp", None, "space", None, None),
            P(),
            P("space", None),
        ),
        check_vma=False,
    )
```

```python
import math

import jax
import jax.numpy as jnp
from jax import lax
from jax.experimental import pallas as pl
from jax.experimental.pallas import tpu as pltpu
from jax.sharding import PartitionSpec as P

root_two_pi = 0.7978845608028654
bf16 = jnp.bfloat16
f32 = jnp.float32
LANES = 128
VMEM_LIMIT = 48 * 1024 * 1024


def call(kernel, outs, scratch, flops, moved, *args):
    whole = pl.BlockSpec(memory_space=pltpu.VMEM)
    return pl.pallas_call(
        kernel,
        out_shape=outs,
        in_specs=[whole] * len(args),
        out_specs=jax.tree.map(lambda _: whole, outs),
        scratch_shapes=scratch,
        compiler_params=pltpu.CompilerParams(vmem_limit_bytes=VMEM_LIMIT),
        cost_estimate=pl.CostEstimate(flops=flops, bytes_accessed=moved, transcendentals=0),
    )(*args)


def column_split(transposed=False):
    size = 2 * LANES
    source = lax.broadcasted_iota(jnp.int32, (size, size), 1 if transposed else 0)
    place = lax.broadcasted_iota(jnp.int32, (size, size), 0 if transposed else 1)
    hit = source == 2 * (place & (LANES - 1)) + (place >> 7)
    return jnp.where(hit, 1.0, 0.0).astype(bf16)


def shifted(even, odd):
    lane = lax.broadcasted_iota(jnp.int32, even.shape, 1)
    odd_before = jnp.where(lane == 0, 0.0, pltpu.roll(odd, 1, 1))
    even_after = jnp.where(lane == LANES - 1, 0.0, pltpu.roll(even, LANES - 1, 1))
    return [odd_before.astype(bf16), even.astype(bf16), odd.astype(bf16), even_after.astype(bf16)]


def send_first(cot_ref, weight_ref, out_ref, wide_ref):
    wide_ref[...] = cot_ref[...].astype(f32)
    weights = weight_ref[...]
    for d in range(16):
        rows = [wide_ref[pl.ds(4 * d + r, 8, stride=64), :] for r in range(4)]
        out_ref[d, :, 0:512] = jnp.concatenate(rows, axis=1).astype(bf16)
        out_ref[d, :, 512:1024] = weights


def tap_weights(weight_ref):
    mid = weight_ref.shape[0]
    lane = lax.broadcasted_iota(jnp.int32, (mid, LANES), 1)
    tiles = [weight_ref[:, LANES * t : LANES * (t + 1)].astype(f32) for t in range(6)]
    tail = weight_ref[:, 768:864].astype(f32)
    tiles.append(jnp.concatenate([tail, jnp.zeros((mid, 32), f32)], axis=1))
    halves = [[], []]
    for ab in range(9):
        first, inset = divmod(96 * ab, LANES)
        rolled = tiles[first] if inset == 0 else pltpu.roll(tiles[first], LANES - inset, 1)
        if inset > 32:
            after = pltpu.roll(tiles[first + 1], LANES - inset, 1)
            rolled = jnp.where(lane < LANES - inset, rolled, after)
        own = jnp.where(lane < 96, rolled, 0.0)
        halves[0].append(own.astype(bf16))
        halves[1].append(pltpu.roll(own, 32, 1).astype(bf16))
    return jnp.concatenate([jnp.concatenate(half, axis=1) for half in halves], axis=0)


def main(before_ref, own_ref, after_ref, got_ref, weight_ref, send_ref, first_ref, last_ref,
         flat_ref, taps_ref, grad_ref, block_ref, pre_grad_ref, conv_ref):
    split = column_split()
    zero = jnp.zeros((LANES, LANES), bf16)
    for plane in range(4):
        taps_ref[plane, 0] = zero
        taps_ref[plane, 9] = zero
    for source, planes in ((own_ref, ((0, 1), (1, 2))), (before_ref, ((1, 0),)), (after_ref, ((0, 3),))):
        columns = jnp.dot(source[...], split, preferred_element_type=f32)
        flat_ref[0] = columns[:, :LANES]
        flat_ref[1] = columns[:, LANES:]
        for z, plane in planes:
            for r in range(8):
                even, odd = (flat_ref[e, pl.ds(8 * z + r, 32, stride=16), :] for e in range(2))
                for v, piece in enumerate(shifted(even, odd)):
                    taps_ref[plane, 1 + r, 32 * v : 32 * v + 32, :] = piece
    got = got_ref[...].reshape(128, 1024)
    cot, filters = got[:, :512], got[:, 512:]
    grad_ref[...] = jnp.dot(filters.astype(f32).T.astype(bf16), cot, preferred_element_type=f32)

    weights = tap_weights(weight_ref)
    for z in range(2):
        for pair in range(4):
            around = []
            for a in range(3):
                for b in range(3):
                    around.append(
                        jnp.concatenate([taps_ref[z + a, 2 * pair + b], taps_ref[z + a, 2 * pair + 1 + b]], axis=1)
                    )
            around = jnp.concatenate(around, axis=0)
            pre = jnp.dot(weights, around, preferred_element_type=f32)
            square = pre * pre
            inner = root_two_pi * pre * (1.0 + 0.044715 * square)
            hyper = jnp.tanh(inner)
            half = 0.5 * (1.0 + hyper)
            hidden = (pre * half).astype(bf16)
            slope = half + 0.5 * pre * (1.0 - hyper * hyper) * (
                root_two_pi + (3.0 * 0.044715 * root_two_pi) * square
            )
            at = 256 * z
            lanes = pl.ds(LANES * pair, LANES)
            block_ref[at : at + 128, lanes] = hidden[:, :LANES]
            block_ref[at + 128 : at + 256, lanes] = hidden[:, LANES:]
            up = jnp.concatenate([grad_ref[at : at + 128, lanes], grad_ref[at + 128 : at + 256, lanes]], axis=1)
            pre_grad = (up * slope).astype(bf16)
            plane_ref = (first_ref, last_ref)[z]
            plane_ref[2 * pair] = pre_grad[:, :LANES]
            plane_ref[2 * pair + 1] = pre_grad[:, LANES:]
            part = lax.dot_general(pre_grad, around, (((1,), (1,)), ((), ())), preferred_element_type=f32)
            if z == 0 and pair == 0:
                conv_ref[...] = part
            else:
                conv_ref[...] += part
    blocks = block_ref[...]
    out = jnp.dot(filters, blocks, preferred_element_type=f32)
    strided = lax.dot_general(cot, blocks, (((1,), (1,)), ((), ())), preferred_element_type=f32)

    lane = lax.broadcasted_iota(jnp.int32, (64, LANES), 1)
    tiles = [jnp.zeros((64, LANES), f32)] * 8
    for ab in range(9):
        lanes = pl.ds(LANES * ab, LANES)
        conv = conv_ref[0:64, lanes] + pltpu.roll(conv_ref[64:128, lanes], 96, 1)
        first, inset = divmod(96 * ab, LANES)
        moved = conv if inset == 0 else pltpu.roll(conv, inset, 1)
        tiles[first] = jnp.where((lane >= inset) & (lane < inset + 96), moved, tiles[first])
        if inset > 32:
            tiles[first + 1] = jnp.where(lane < inset - 32, moved, tiles[first + 1])
    conv = jnp.concatenate(tiles, axis=1)
    for j in range(16):
        rows, group, side = 8 * j, 8 * (j // 2), 512 * (j % 2)
        piece = jnp.concatenate(
            [out[rows : rows + 8], strided[rows : rows + 8], conv[group : group + 8, side : side + 512]], axis=0
        )
        send_ref[j] = piece.astype(bf16)


def back_weights(weight_ref):
    wide = weight_ref[...].astype(f32)
    turned = jnp.concatenate([wide, wide], axis=0).T
    lane = lax.broadcasted_iota(jnp.int32, (32, LANES), 1)
    low = lane < 64
    pieces = []
    for a in range(3):
        for b in range(3):
            at = 32 * 3 * (3 * (2 - a) + 2 - b)
            tap = [turned[at + 32 * e : at + 32 * e + 32] for e in range(3)]
            even = [jnp.where(low, tap[2], tap[1]), jnp.where(low, tap[0], 0.0)]
            odd = [jnp.where(low, 0.0, tap[2]), jnp.where(low, tap[1], tap[0])]
            pieces.append(
                jnp.concatenate([jnp.concatenate(even, axis=1), jnp.concatenate(odd, axis=1)], axis=0).astype(bf16)
            )
    return jnp.concatenate(pieces, axis=1)


def back(before_ref, first_ref, last_ref, after_ref, weight_ref, out_ref, taps_ref, turn_ref, flat_ref):
    zero = jnp.zeros((256, LANES), bf16)
    for plane, source in enumerate((before_ref, first_ref, last_ref, after_ref)):
        taps_ref[plane, 0] = zero
        taps_ref[plane, 9] = zero
        for r in range(8):
            cells = source[r].astype(f32)
            for v, piece in enumerate(shifted(cells[:64], cells[64:])):
                taps_ref[plane, 1 + r, 64 * v : 64 * v + 64, :] = piece
    weights = back_weights(weight_ref)
    for z in range(2):
        for pair in range(4):
            around = []
            for a in range(3):
                for b in range(3):
                    around.append(
                        jnp.concatenate([taps_ref[z + a, 2 * pair + b], taps_ref[z + a, 2 * pair + 1 + b]], axis=1)
                    )
            grad = jnp.dot(weights, jnp.concatenate(around, axis=0), preferred_element_type=f32).astype(bf16)
            for side in range(2):
                row = 8 * z + 2 * pair + side
                lanes = slice(LANES * side, LANES * side + LANES)
                turn_ref[32 * row : 32 * row + 32, :] = jnp.concatenate([grad[:32, lanes], grad[32:, lanes]], axis=1)
    columns = jnp.dot(turn_ref[...], column_split(True), preferred_element_type=f32)
    for row in range(16):
        for side in range(2):
            flat_ref[side, pl.ds(row, 32, stride=16), :] = columns[
                32 * row : 32 * row + 32, LANES * side : LANES * side + LANES
            ]
    for side in range(2):
        out_ref[:, LANES * side : LANES * side + LANES] = flat_ref[side].astype(bf16)


def sum_space(got_ref, send_ref):
    total = got_ref[0, 8:24, :].astype(f32)
    for j in range(1, 16):
        total = total + got_ref[j, 8:24, :].astype(f32)
    total = total.astype(bf16)
    for j in range(16):
        send_ref[j] = total


def place_output(got_ref, out_ref, wide_ref):
    for d in range(16):
        for r in range(4):
            wide_ref[pl.ds(4 * d + r, 8, stride=64), :] = got_ref[d, 0:8, LANES * r : LANES * r + LANES].astype(f32)
    out_ref[...] = wide_ref[...].astype(bf16)


def sum_samples(strided_scale, conv_scale, got_ref, strided_ref, send_ref):
    total = got_ref[0].astype(f32)
    for j in range(1, 16):
        total = total + got_ref[j].astype(f32)
    strided_ref[...] = total[:8] * strided_scale
    conv = (total[8:] * conv_scale).astype(bf16)
    for j in range(16):
        send_ref[j] = conv


def place_conv(got_ref, out_ref):
    for j in range(16):
        rows, side = 8 * (j // 2), 512 * (j % 2)
        width = min(512, 864 - side)
        out_ref[rows : rows + 8, side : side + width] = got_ref[j, :, :width].astype(f32)


def shards(volume, conv_weight, strided_weight, cotangent):
    depth = volume.shape[2]
    n_space, n_dp = lax.axis_size("space"), lax.axis_size("dp")
    cells = n_dp * depth * n_space * volume.shape[3] * volume.shape[4]
    ends = n_space - 1
    up = [(i, i + 1) for i in range(ends)]
    down = [(i + 1, i) for i in range(ends)]

    def shape(dims, dtype):
        return jax.ShapeDtypeStruct(dims, dtype)

    send = call(
        send_first, shape((16, 8, 1024), bf16), [pltpu.VMEM((512, LANES), f32)], 0, 400_000,
        cotangent.reshape(512, LANES), strided_weight,
    )
    got = lax.all_to_all(send, "space", 0, 0, tiled=True)
    before = lax.ppermute(volume, "space", up).reshape(512, 256)
    after = lax.ppermute(volume, "space", down).reshape(512, 256)
    plane = shape((8, LANES, LANES), bf16)
    send, first, last = call(
        main, (shape((16, 24, 512), bf16), plane, plane),
        [
            pltpu.VMEM((2, 512, LANES), f32),
            pltpu.VMEM((4, 10, LANES, LANES), bf16),
            pltpu.VMEM((512, 512), f32),
            pltpu.VMEM((512, 512), bf16),
            pltpu.VMEM((8, LANES, LANES), bf16),
            pltpu.VMEM((LANES, 9 * LANES), f32),
        ],
        2_000_000_000, 2_000_000,
        before, volume.reshape(512, 256), after, got, conv_weight,
    )
    got = lax.all_to_all(send, "space", 0, 0, tiled=True)
    grad_before = lax.ppermute(last, "space", up)
    grad_after = lax.ppermute(first, "space", down)
    send = call(sum_space, shape((16, 16, 512), bf16), [], 0, 600_000, got)
    output = call(place_output, shape((512, LANES), bf16), [pltpu.VMEM((512, LANES), f32)], 0, 600_000, got)
    got = lax.all_to_all(send, "dp", 0, 0, tiled=True)
    strided_grad, send = call(
        lambda *refs: sum_samples(1.0 / math.sqrt(cells / 8), 1.0 / math.sqrt(cells), *refs),
        (shape((8, 512), f32), shape((16, 8, 512), bf16)), [], 0, 600_000, got,
    )
    got = lax.all_to_all(send, "space", 0, 0, tiled=True)
    conv_grad = call(place_conv, shape((64, 864), f32), [], 0, 300_000, got)
    vol_grad = call(
        back, shape((512, 256), bf16),
        [
            pltpu.VMEM((4, 10, 256, LANES), bf16),
            pltpu.VMEM((512, 256), bf16),
            pltpu.VMEM((2, 512, LANES), f32),
        ],
        2_000_000_000, 2_000_000,
        grad_before, first, last, grad_after, conv_weight,
    )
    return output.reshape(cotangent.shape), vol_grad.reshape(volume.shape), conv_grad, strided_grad


def solution(mesh):
    return jax.shard_map(
        shards,
        mesh=mesh,
        in_specs=(
            P("dp", None, "space", None, None),
            P(),
            P("space", None),
            P("dp", "space", None, None, None),
        ),
        out_specs=(
            P("dp", "space", None, None, None),
            P("dp", None, "space", None, None),
            P(),
            P("space", None),
        ),
        check_vma=False,
    )
```

```python
import math

import jax
import jax.numpy as jnp
from jax import lax
from jax.experimental import pallas as pl
from jax.experimental.pallas import tpu as pltpu
from jax.sharding import PartitionSpec as P

root_two_pi = 0.7978845608028654
bf16 = jnp.bfloat16
f32 = jnp.float32
LANES = 128
VMEM_LIMIT = 16 * 1024 * 1024


def call(kernel, outs, scratch, flops, moved, *args, space=pltpu.VMEM):
    whole = pl.BlockSpec(memory_space=pltpu.VMEM)
    return pl.pallas_call(
        kernel,
        out_shape=outs,
        in_specs=[pl.BlockSpec(memory_space=space)] * len(args),
        out_specs=jax.tree.map(lambda _: whole, outs),
        scratch_shapes=scratch,
        compiler_params=pltpu.CompilerParams(vmem_limit_bytes=VMEM_LIMIT),
        cost_estimate=pl.CostEstimate(flops=flops, bytes_accessed=moved, transcendentals=0),
    )(*args)


def column_split(transposed=False):
    size = 2 * LANES
    source = lax.broadcasted_iota(jnp.int32, (size, size), 1 if transposed else 0)
    place = lax.broadcasted_iota(jnp.int32, (size, size), 0 if transposed else 1)
    hit = source == 2 * (place & (LANES - 1)) + (place >> 7)
    return jnp.where(hit, 1.0, 0.0).astype(bf16)


def shifted(even, odd):
    lane = lax.broadcasted_iota(jnp.int32, even.shape, 1)
    odd_before = jnp.where(lane == 0, 0.0, pltpu.roll(odd, 1, 1))
    even_after = jnp.where(lane == LANES - 1, 0.0, pltpu.roll(even, LANES - 1, 1))
    return [odd_before.astype(bf16), even.astype(bf16), odd.astype(bf16), even_after.astype(bf16)]


def core_index():
    return lax.rem(lax.axis_index("space"), 2)


def send_first(cot_hbm, weight_hbm, out_ref, cot_ref, weight_ref, wide_ref, sems):
    copies = [
        pltpu.make_async_copy(source, target, sems.at[i])
        for i, (source, target) in enumerate(((cot_hbm, cot_ref), (weight_hbm, weight_ref)))
    ]
    for copy in copies:
        copy.start()
    for copy in copies:
        copy.wait()
    wide_ref[...] = cot_ref[...].astype(f32)
    weights = weight_ref[...]
    for d in range(16):
        rows = [wide_ref[pl.ds(4 * d + r, 8, stride=64), :] for r in range(4)]
        out_ref[d, :, 0:512] = jnp.concatenate(rows, axis=1).astype(bf16)
        out_ref[d, :, 512:1024] = weights


def split_columns(own_ref, across_ref, inside_ref, flat_ref, planes_ref):
    columns = jnp.dot(own_ref[...], column_split(), preferred_element_type=f32)
    for e in range(2):
        flat_ref[e] = columns[:, LANES * e : LANES * e + LANES]
    for z in range(2):
        for r in range(8):
            for e in range(2):
                cells = flat_ref[e, pl.ds(8 * z + r, 32, stride=16), :]
                planes_ref[z, r, 32 * e : 32 * e + 32, :] = cells.astype(bf16)
    core = core_index()
    across_ref[...] = planes_ref[core]
    inside_ref[...] = planes_ref[1 - core]


def tap_weights(weight_ref):
    mid = weight_ref.shape[0]
    lane = lax.broadcasted_iota(jnp.int32, (mid, LANES), 1)
    tiles = [weight_ref[:, LANES * t : LANES * (t + 1)].astype(f32) for t in range(6)]
    tail = weight_ref[:, 768:864].astype(f32)
    tiles.append(jnp.concatenate([tail, jnp.zeros((mid, 32), f32)], axis=1))
    halves = [[], []]
    for ab in range(9):
        first, inset = divmod(96 * ab, LANES)
        rolled = tiles[first] if inset == 0 else pltpu.roll(tiles[first], LANES - inset, 1)
        if inset > 32:
            after = pltpu.roll(tiles[first + 1], LANES - inset, 1)
            rolled = jnp.where(lane < LANES - inset, rolled, after)
        own = jnp.where(lane < 96, rolled, 0.0)
        halves[0].append(own.astype(bf16))
        halves[1].append(pltpu.roll(own, 32, 1).astype(bf16))
    return jnp.concatenate([jnp.concatenate(half, axis=1) for half in halves], axis=0)


def fill_taps(taps_ref, planes):
    size = taps_ref.shape[2] // 4
    zero = jnp.zeros(taps_ref.shape[2:], bf16)
    for plane, source in planes:
        taps_ref[plane, 0] = zero
        taps_ref[plane, 9] = zero
        for r in range(8):
            cells = source[r].astype(f32)
            for v, piece in enumerate(shifted(cells[:size], cells[size:])):
                taps_ref[plane, 1 + r, size * v : size * v + size, :] = piece


def surroundings(taps_ref, planes, pair):
    return jnp.concatenate(
        [
            jnp.concatenate([taps_ref[plane, 2 * pair + b], taps_ref[plane, 2 * pair + 1 + b]], axis=1)
            for plane in planes
            for b in range(3)
        ],
        axis=0,
    )


def one_plane(z, planes, got_ref, weight_ref, taps_ref, grad_ref, block_ref, grad_plane_ref, conv_ref):
    fill_taps(taps_ref, planes)
    cot = got_ref[:, :, 0:512].reshape(128, 512)
    filters = got_ref[:, :, pl.ds(pl.multiple_of(512 + 256 * z, 256), 256)].reshape(128, 256)
    grad_ref[...] = jnp.dot(filters.astype(f32).T.astype(bf16), cot, preferred_element_type=f32)
    weights = tap_weights(weight_ref)
    for pair in range(4):
        around = surroundings(taps_ref, range(3), pair)
        pre = jnp.dot(weights, around, preferred_element_type=f32)
        square = pre * pre
        inner = root_two_pi * pre * (1.0 + 0.044715 * square)
        hyper = jnp.tanh(inner)
        half = 0.5 * (1.0 + hyper)
        hidden = (pre * half).astype(bf16)
        slope = half + 0.5 * pre * (1.0 - hyper * hyper) * (root_two_pi + (3.0 * 0.044715 * root_two_pi) * square)
        halves = []
        for side in range(2):
            rows = slice(128 * side, 128 * side + 128)
            columns = slice(LANES * pair, LANES * pair + LANES)
            lanes = slice(LANES * side, LANES * side + LANES)
            block_ref[rows, columns] = hidden[:, lanes]
            halves.append((grad_ref[rows, columns] * slope[:, lanes]).astype(bf16))
            grad_plane_ref[2 * pair + side] = halves[side]
        part = lax.dot_general(
            jnp.concatenate(halves, axis=1), around, (((1,), (1,)), ((), ())), preferred_element_type=f32
        )
        if pair == 0:
            conv_ref[...] = part
        else:
            conv_ref[...] += part
    blocks = block_ref[...]
    out = jnp.dot(filters, blocks, preferred_element_type=f32)
    strided = lax.dot_general(cot, blocks, (((1,), (1,)), ((), ())), preferred_element_type=f32)
    return out, strided


def inside(across_own, inside_own, inside_got, got_ref, weight_ref, grad_plane_ref, conv_ref, out_ref, strided_ref,
           taps_ref, grad_ref, block_ref):
    core = core_index()
    out, strided = one_plane(
        1 - core, ((2 * core, across_own), (1, inside_own), (2 - 2 * core, inside_got)),
        got_ref, weight_ref, taps_ref, grad_ref, block_ref, grad_plane_ref, conv_ref,
    )
    out_ref[...] = out
    strided_ref[...] = strided


def across(across_got, across_own, inside_own, got_ref, weight_ref, conv_in, out_in, strided_in, send_ref, grad_plane_ref,
           taps_ref, grad_ref, block_ref, conv_ref):
    core = core_index()
    out, strided = one_plane(
        core, ((2 * core, across_got), (1, across_own), (2 - 2 * core, inside_own)),
        got_ref, weight_ref, taps_ref, grad_ref, block_ref, grad_plane_ref, conv_ref,
    )
    out = out + out_in[...]
    other = strided_in[...]
    strided = jnp.concatenate(
        [jnp.where(core == 0, strided, other), jnp.where(core == 0, other, strided)], axis=1
    )
    lane = lax.broadcasted_iota(jnp.int32, (64, LANES), 1)
    tiles = [jnp.zeros((64, LANES), f32)] * 8
    for ab in range(9):
        lanes = pl.ds(LANES * ab, LANES)
        even = conv_ref[0:64, lanes] + conv_in[0:64, lanes]
        odd = conv_ref[64:128, lanes] + conv_in[64:128, lanes]
        conv = even + pltpu.roll(odd, 96, 1)
        first, inset = divmod(96 * ab, LANES)
        moved = conv if inset == 0 else pltpu.roll(conv, inset, 1)
        tiles[first] = jnp.where((lane >= inset) & (lane < inset + 96), moved, tiles[first])
        if inset > 32:
            tiles[first + 1] = jnp.where(lane < inset - 32, moved, tiles[first + 1])
    conv = jnp.concatenate(tiles, axis=1)
    for j in range(16):
        rows, group, side = 8 * j, 8 * (j // 2), 512 * (j % 2)
        piece = jnp.concatenate(
            [out[rows : rows + 8], strided[rows : rows + 8], conv[group : group + 8, side : side + 512]], axis=0
        )
        send_ref[j] = piece.astype(bf16)


def back_weights(weight_ref):
    wide = weight_ref[...].astype(f32)
    turned = jnp.concatenate([wide, wide], axis=0).T
    lane = lax.broadcasted_iota(jnp.int32, (32, LANES), 1)
    low = lane < 64
    pieces = []
    for a in range(3):
        for b in range(3):
            at = 32 * 3 * (3 * (2 - a) + 2 - b)
            tap = [turned[at + 32 * e : at + 32 * e + 32] for e in range(3)]
            even = [jnp.where(low, tap[2], tap[1]), jnp.where(low, tap[0], 0.0)]
            odd = [jnp.where(low, 0.0, tap[2]), jnp.where(low, tap[1], tap[0])]
            pieces.append(
                jnp.concatenate([jnp.concatenate(even, axis=1), jnp.concatenate(odd, axis=1)], axis=0).astype(bf16)
            )
    return jnp.concatenate(pieces, axis=1)


def back(across_own, inside_own, weight_ref, own_ref, across_ref, inside_ref, taps_ref, ends_ref):
    core = core_index()
    fill_taps(taps_ref, ((core, across_own), (1 - core, inside_own)))
    weights = back_weights(weight_ref)
    for plane in range(-1, 3):
        sources = [z for z in range(2) if 0 <= z - plane + 1 < 3]
        depth = sources[0] - plane + 1
        columns = weights[:, 768 * depth : 768 * (depth + len(sources))]
        for pair in range(4):
            grad = jnp.dot(columns, surroundings(taps_ref, sources, pair), preferred_element_type=f32)
            for side in range(2):
                part = grad[:, LANES * side : LANES * side + LANES]
                if 0 <= plane < 2:
                    own_ref[plane, 2 * pair + side] = part
                else:
                    ends_ref[(plane + 1) // 3, 2 * pair + side] = part.astype(bf16)
    across_ref[...] = ends_ref[core]
    inside_ref[...] = ends_ref[1 - core]


def finish(own_ref, across_got, inside_got, out_ref, sum_ref, turn_ref, flat_ref):
    core = core_index()
    sum_ref[core] = own_ref[core] + across_got[...].astype(f32)
    sum_ref[1 - core] = own_ref[1 - core] + inside_got[...].astype(f32)
    for row in range(16):
        grad = sum_ref[row // 8, row % 8].astype(bf16)
        turn_ref[32 * row : 32 * row + 32, :] = jnp.concatenate([grad[:32], grad[32:]], axis=1)
    columns = jnp.dot(turn_ref[...], column_split(True), preferred_element_type=f32)
    for row in range(16):
        for side in range(2):
            flat_ref[side, pl.ds(row, 32, stride=16), :] = columns[
                32 * row : 32 * row + 32, LANES * side : LANES * side + LANES
            ]
    for side in range(2):
        out_ref[:, LANES * side : LANES * side + LANES] = flat_ref[side].astype(bf16)


def sum_space(got_ref, send_ref):
    total = got_ref[0, 8:24, :].astype(f32)
    for j in range(1, 16):
        total = total + got_ref[j, 8:24, :].astype(f32)
    total = total.astype(bf16)
    for j in range(16):
        send_ref[j] = total


def place_output(got_ref, out_ref, wide_ref):
    for d in range(16):
        for r in range(4):
            wide_ref[pl.ds(4 * d + r, 8, stride=64), :] = got_ref[d, 0:8, LANES * r : LANES * r + LANES].astype(f32)
    out_ref[...] = wide_ref[...].astype(bf16)


def sum_samples(strided_scale, conv_scale, got_ref, strided_ref, send_ref):
    total = got_ref[0].astype(f32)
    for j in range(1, 16):
        total = total + got_ref[j].astype(f32)
    strided_ref[...] = total[:8] * strided_scale
    conv = (total[8:] * conv_scale).astype(bf16)
    for j in range(16):
        send_ref[j] = conv


def place_conv(got_ref, out_ref):
    for j in range(16):
        rows, side = 8 * (j // 2), 512 * (j % 2)
        width = min(512, 864 - side)
        out_ref[rows : rows + 8, side : side + width] = got_ref[j, :, :width].astype(f32)


def shards(volume, conv_weight, strided_weight, cotangent):
    depth = volume.shape[2]
    n_space, n_dp = lax.axis_size("space"), lax.axis_size("dp")
    cells = n_dp * depth * n_space * volume.shape[3] * volume.shape[4]
    between_chips = [pair for i in range(1, n_space - 1, 2) for pair in ((i, i + 1), (i + 1, i))]
    in_chip = [pair for i in range(0, n_space, 2) for pair in ((i, i + 1), (i + 1, i))]

    def shape(dims, dtype):
        return jax.ShapeDtypeStruct(dims, dtype)

    plane = shape((8, 64, LANES), bf16)
    send = call(
        send_first, shape((16, 8, 1024), bf16),
        [
            pltpu.VMEM((512, LANES), bf16),
            pltpu.VMEM((8, 512), bf16),
            pltpu.VMEM((512, LANES), f32),
            pltpu.SemaphoreType.DMA((2,)),
        ],
        0, 400_000,
        *(pltpu.with_memory_space_constraint(x, pltpu.HBM) for x in (cotangent.reshape(512, LANES), strided_weight)),
        space=pltpu.HBM,
    )
    got = lax.all_to_all(send, "space", 0, 0, tiled=True)
    cells_in, _ = lax.optimization_barrier((volume, send))
    across_vol, inside_vol = call(
        split_columns, (plane, plane),
        [pltpu.VMEM((2, 512, LANES), f32), pltpu.VMEM((2, 8, 64, LANES), bf16)], 4_000_000_000, 2_000_000,
        cells_in.reshape(512, 256),
    )
    across_got = lax.ppermute(across_vol, "space", between_chips)
    inside_got = lax.ppermute(inside_vol, "space", in_chip)
    grad_plane = shape((8, LANES, LANES), bf16)
    scratch = [pltpu.VMEM((3, 10, LANES, LANES), bf16), pltpu.VMEM((256, 512), f32), pltpu.VMEM((256, 512), bf16)]
    inside_grad, conv_terms, out_terms, strided_terms = call(
        inside,
        (grad_plane, shape((LANES, 9 * LANES), f32), shape((LANES, 512), f32), shape((LANES, 256), f32)),
        scratch, 3_000_000_000, 2_000_000,
        across_vol, inside_vol, inside_got, got, conv_weight,
    )
    send, across_grad = call(
        across, (shape((16, 24, 512), bf16), grad_plane),
        scratch + [pltpu.VMEM((LANES, 9 * LANES), f32)], 3_000_000_000, 3_000_000,
        across_got, across_vol, inside_vol, got, conv_weight, conv_terms, out_terms, strided_terms,
    )
    got = lax.all_to_all(send, "space", 0, 0, tiled=True)
    own_terms, across_terms, inside_terms = call(
        back, (shape((2, 8, 64, LANES), f32), plane, plane),
        [pltpu.VMEM((2, 10, 256, LANES), bf16), pltpu.VMEM((2, 8, 64, LANES), bf16)],
        3_000_000_000, 3_000_000,
        across_grad, inside_grad, conv_weight,
    )
    got, own_terms, across_terms, inside_terms = lax.optimization_barrier(
        (got, own_terms, across_terms, inside_terms)
    )
    across_got = lax.ppermute(across_terms, "space", between_chips)
    inside_got = lax.ppermute(inside_terms, "space", in_chip)
    send = call(sum_space, shape((16, 16, 512), bf16), [], 0, 600_000, got)
    output = call(place_output, shape((512, LANES), bf16), [pltpu.VMEM((512, LANES), f32)], 0, 600_000, got)
    got = lax.all_to_all(send, "dp", 0, 0, tiled=True)
    strided_grad, send = call(
        lambda *refs: sum_samples(1.0 / math.sqrt(cells / 8), 1.0 / math.sqrt(cells), *refs),
        (shape((8, 512), f32), shape((16, 8, 512), bf16)), [], 0, 600_000, got,
    )
    got = lax.all_to_all(send, "space", 0, 0, tiled=True)
    vol_grad = call(
        finish, shape((512, 256), bf16),
        [
            pltpu.VMEM((2, 8, 64, LANES), f32),
            pltpu.VMEM((512, 256), bf16),
            pltpu.VMEM((2, 512, LANES), f32),
        ],
        1_000_000_000, 2_000_000,
        own_terms, across_got, inside_got,
    )
    conv_grad = call(place_conv, shape((64, 864), f32), [], 0, 300_000, got)
    return output.reshape(cotangent.shape), vol_grad.reshape(volume.shape), conv_grad, strided_grad


def solution(mesh):
    return jax.shard_map(
        shards,
        mesh=mesh,
        in_specs=(
            P("dp", None, "space", None, None),
            P(),
            P("space", None),
            P("dp", "space", None, None, None),
        ),
        out_specs=(
            P("dp", "space", None, None, None),
            P("dp", None, "space", None, None),
            P(),
            P("space", None),
        ),
        check_vma=False,
    )
```

```python
import math

import jax
import jax.numpy as jnp
from jax import lax
from jax.experimental import pallas as pl
from jax.experimental.pallas import tpu as pltpu
from jax.sharding import PartitionSpec as P

root_two_pi = 0.7978845608028654
bf16 = jnp.bfloat16
f32 = jnp.float32
LANES = 128


def rank_order(bits, reverse):
    order = [sum(((rank >> k) & 1) << bit for k, bit in enumerate(bits)) for rank in range(16)]
    return order[::-1] if reverse else order


ORDER_IN = rank_order((1, 2, 3, 0), True)
ORDER_SLABS = rank_order((1, 2, 3, 0), False)
ORDER_SAMPLES = rank_order((3, 0, 1, 2), True)
ORDER_OUT = rank_order((1, 2, 3, 0), True)
VMEM_LIMIT = 16 * 1024 * 1024


def call(kernel, outs, scratch, flops, moved, *args, space=pltpu.VMEM):
    whole = pl.BlockSpec(memory_space=pltpu.VMEM)
    return pl.pallas_call(
        kernel,
        out_shape=outs,
        in_specs=[pl.BlockSpec(memory_space=space)] * len(args),
        out_specs=jax.tree.map(lambda _: whole, outs),
        scratch_shapes=scratch,
        compiler_params=pltpu.CompilerParams(vmem_limit_bytes=VMEM_LIMIT),
        cost_estimate=pl.CostEstimate(flops=flops, bytes_accessed=moved, transcendentals=0),
    )(*args)


def column_split(transposed=False):
    size = 2 * LANES
    source = lax.broadcasted_iota(jnp.int32, (size, size), 1 if transposed else 0)
    place = lax.broadcasted_iota(jnp.int32, (size, size), 0 if transposed else 1)
    hit = source == 2 * (place & (LANES - 1)) + (place >> 7)
    return jnp.where(hit, 1.0, 0.0).astype(bf16)


def shifted(even, odd):
    lane = lax.broadcasted_iota(jnp.int32, even.shape, 1)
    odd_before = jnp.where(lane == 0, 0.0, pltpu.roll(odd, 1, 1))
    even_after = jnp.where(lane == LANES - 1, 0.0, pltpu.roll(even, LANES - 1, 1))
    return [odd_before.astype(bf16), even.astype(bf16), odd.astype(bf16), even_after.astype(bf16)]


def core_index():
    return lax.rem(lax.axis_index("space"), 2)


def send_first(cot_hbm, weight_hbm, out_ref, cot_ref, weight_ref, wide_ref, sems):
    copies = [
        pltpu.make_async_copy(source, target, sems.at[i])
        for i, (source, target) in enumerate(((cot_hbm, cot_ref), (weight_hbm, weight_ref)))
    ]
    for copy in copies:
        copy.start()
    for copy in copies:
        copy.wait()
    wide_ref[...] = cot_ref[...].astype(f32)
    weights = weight_ref[...]
    for slot, d in enumerate(ORDER_IN):
        rows = [wide_ref[pl.ds(4 * d + r, 8, stride=64), :] for r in range(4)]
        out_ref[slot, :, 0:512] = jnp.concatenate(rows, axis=1).astype(bf16)
        out_ref[slot, :, 512:1024] = weights


def split_columns(own_ref, across_ref, inside_ref, flat_ref, planes_ref):
    columns = jnp.dot(own_ref[...], column_split(), preferred_element_type=f32)
    for e in range(2):
        flat_ref[e] = columns[:, LANES * e : LANES * e + LANES]
    for z in range(2):
        for r in range(8):
            for e in range(2):
                cells = flat_ref[e, pl.ds(8 * z + r, 32, stride=16), :]
                planes_ref[z, r, 32 * e : 32 * e + 32, :] = cells.astype(bf16)
    core = core_index()
    across_ref[...] = planes_ref[core]
    inside_ref[...] = planes_ref[1 - core]


def tap_weights(weight_ref):
    mid = weight_ref.shape[0]
    lane = lax.broadcasted_iota(jnp.int32, (mid, LANES), 1)
    tiles = [weight_ref[:, LANES * t : LANES * (t + 1)].astype(f32) for t in range(6)]
    tail = weight_ref[:, 768:864].astype(f32)
    tiles.append(jnp.concatenate([tail, jnp.zeros((mid, 32), f32)], axis=1))
    halves = [[], []]
    for ab in range(9):
        first, inset = divmod(96 * ab, LANES)
        rolled = tiles[first] if inset == 0 else pltpu.roll(tiles[first], LANES - inset, 1)
        if inset > 32:
            after = pltpu.roll(tiles[first + 1], LANES - inset, 1)
            rolled = jnp.where(lane < LANES - inset, rolled, after)
        own = jnp.where(lane < 96, rolled, 0.0)
        halves[0].append(own.astype(bf16))
        halves[1].append(pltpu.roll(own, 32, 1).astype(bf16))
    return jnp.concatenate([jnp.concatenate(half, axis=1) for half in halves], axis=0)


def fill_taps(taps_ref, planes):
    size = taps_ref.shape[2] // 4
    zero = jnp.zeros(taps_ref.shape[2:], bf16)
    for plane, source in planes:
        taps_ref[plane, 0] = zero
        taps_ref[plane, 9] = zero
        for r in range(8):
            cells = source[r].astype(f32)
            for v, piece in enumerate(shifted(cells[:size], cells[size:])):
                taps_ref[plane, 1 + r, size * v : size * v + size, :] = piece


def surroundings(taps_ref, planes, pair):
    return jnp.concatenate(
        [
            jnp.concatenate([taps_ref[plane, 2 * pair + b], taps_ref[plane, 2 * pair + 1 + b]], axis=1)
            for plane in planes
            for b in range(3)
        ],
        axis=0,
    )


def one_plane(z, planes, got_ref, weight_ref, taps_ref, grad_ref, block_ref, grad_plane_ref, conv_ref):
    fill_taps(taps_ref, planes)
    cot = got_ref[:, :, 0:512].reshape(128, 512)
    filters = got_ref[:, :, pl.ds(pl.multiple_of(512 + 256 * z, 256), 256)].reshape(128, 256)
    grad_ref[...] = jnp.dot(filters.astype(f32).T.astype(bf16), cot, preferred_element_type=f32)
    weights = tap_weights(weight_ref)
    for pair in range(4):
        around = surroundings(taps_ref, range(3), pair)
        pre = jnp.dot(weights, around, preferred_element_type=f32)
        square = pre * pre
        inner = root_two_pi * pre * (1.0 + 0.044715 * square)
        hyper = jnp.tanh(inner)
        half = 0.5 * (1.0 + hyper)
        hidden = (pre * half).astype(bf16)
        slope = half + 0.5 * pre * (1.0 - hyper * hyper) * (root_two_pi + (3.0 * 0.044715 * root_two_pi) * square)
        halves = []
        for side in range(2):
            rows = slice(128 * side, 128 * side + 128)
            columns = slice(LANES * pair, LANES * pair + LANES)
            lanes = slice(LANES * side, LANES * side + LANES)
            block_ref[rows, columns] = hidden[:, lanes]
            halves.append((grad_ref[rows, columns] * slope[:, lanes]).astype(bf16))
            grad_plane_ref[2 * pair + side] = halves[side]
        part = lax.dot_general(
            jnp.concatenate(halves, axis=1), around, (((1,), (1,)), ((), ())), preferred_element_type=f32
        )
        if pair == 0:
            conv_ref[...] = part
        else:
            conv_ref[...] += part
    blocks = block_ref[...]
    out = jnp.dot(filters, blocks, preferred_element_type=f32)
    strided = lax.dot_general(cot, blocks, (((1,), (1,)), ((), ())), preferred_element_type=f32)
    return out, strided


def inside(across_own, inside_own, inside_got, got_ref, weight_ref, grad_plane_ref, conv_ref, out_ref, strided_ref,
           taps_ref, grad_ref, block_ref):
    core = core_index()
    out, strided = one_plane(
        1 - core, ((2 * core, across_own), (1, inside_own), (2 - 2 * core, inside_got)),
        got_ref, weight_ref, taps_ref, grad_ref, block_ref, grad_plane_ref, conv_ref,
    )
    out_ref[...] = out
    strided_ref[...] = strided


def across(across_got, across_own, inside_own, got_ref, weight_ref, conv_in, out_in, strided_in, send_ref, grad_plane_ref,
           taps_ref, grad_ref, block_ref, conv_ref):
    core = core_index()
    out, strided = one_plane(
        core, ((2 * core, across_got), (1, across_own), (2 - 2 * core, inside_own)),
        got_ref, weight_ref, taps_ref, grad_ref, block_ref, grad_plane_ref, conv_ref,
    )
    out = out + out_in[...]
    other = strided_in[...]
    strided = jnp.concatenate(
        [jnp.where(core == 0, strided, other), jnp.where(core == 0, other, strided)], axis=1
    )
    lane = lax.broadcasted_iota(jnp.int32, (64, LANES), 1)
    tiles = [jnp.zeros((64, LANES), f32)] * 8
    for ab in range(9):
        lanes = pl.ds(LANES * ab, LANES)
        even = conv_ref[0:64, lanes] + conv_in[0:64, lanes]
        odd = conv_ref[64:128, lanes] + conv_in[64:128, lanes]
        conv = even + pltpu.roll(odd, 96, 1)
        first, inset = divmod(96 * ab, LANES)
        moved = conv if inset == 0 else pltpu.roll(conv, inset, 1)
        tiles[first] = jnp.where((lane >= inset) & (lane < inset + 96), moved, tiles[first])
        if inset > 32:
            tiles[first + 1] = jnp.where(lane < inset - 32, moved, tiles[first + 1])
    conv = jnp.concatenate(tiles, axis=1)
    for slot, j in enumerate(ORDER_SLABS):
        rows, group, side = 8 * ORDER_IN.index(j), 8 * (j // 2), 512 * (j % 2)
        piece = jnp.concatenate(
            [out[rows : rows + 8], strided[rows : rows + 8], conv[group : group + 8, side : side + 512]], axis=0
        )
        send_ref[slot] = piece.astype(bf16)


def back_weights(weight_ref):
    wide = weight_ref[...].astype(f32)
    turned = jnp.concatenate([wide, wide], axis=0).T
    lane = lax.broadcasted_iota(jnp.int32, (32, LANES), 1)
    low = lane < 64
    pieces = []
    for a in range(3):
        for b in range(3):
            at = 32 * 3 * (3 * (2 - a) + 2 - b)
            tap = [turned[at + 32 * e : at + 32 * e + 32] for e in range(3)]
            even = [jnp.where(low, tap[2], tap[1]), jnp.where(low, tap[0], 0.0)]
            odd = [jnp.where(low, 0.0, tap[2]), jnp.where(low, tap[1], tap[0])]
            pieces.append(
                jnp.concatenate([jnp.concatenate(even, axis=1), jnp.concatenate(odd, axis=1)], axis=0).astype(bf16)
            )
    return jnp.concatenate(pieces, axis=1)


def back(across_own, inside_own, weight_ref, own_ref, across_ref, inside_ref, taps_ref, ends_ref):
    core = core_index()
    fill_taps(taps_ref, ((core, across_own), (1 - core, inside_own)))
    weights = back_weights(weight_ref)
    for plane in range(-1, 3):
        sources = [z for z in range(2) if 0 <= z - plane + 1 < 3]
        depth = sources[0] - plane + 1
        columns = weights[:, 768 * depth : 768 * (depth + len(sources))]
        for pair in range(4):
            grad = jnp.dot(columns, surroundings(taps_ref, sources, pair), preferred_element_type=f32)
            for side in range(2):
                part = grad[:, LANES * side : LANES * side + LANES]
                if 0 <= plane < 2:
                    own_ref[plane, 2 * pair + side] = part
                else:
                    ends_ref[(plane + 1) // 3, 2 * pair + side] = part.astype(bf16)
    across_ref[...] = ends_ref[core]
    inside_ref[...] = ends_ref[1 - core]


def finish(own_ref, across_got, inside_got, out_ref, sum_ref, turn_ref, flat_ref):
    core = core_index()
    sum_ref[core] = own_ref[core] + across_got[...].astype(f32)
    sum_ref[1 - core] = own_ref[1 - core] + inside_got[...].astype(f32)
    for row in range(16):
        grad = sum_ref[row // 8, row % 8].astype(bf16)
        turn_ref[32 * row : 32 * row + 32, :] = jnp.concatenate([grad[:32], grad[32:]], axis=1)
    columns = jnp.dot(turn_ref[...], column_split(True), preferred_element_type=f32)
    for row in range(16):
        for side in range(2):
            flat_ref[side, pl.ds(row, 32, stride=16), :] = columns[
                32 * row : 32 * row + 32, LANES * side : LANES * side + LANES
            ]
    for side in range(2):
        out_ref[:, LANES * side : LANES * side + LANES] = flat_ref[side].astype(bf16)


def sum_space(got_ref, send_ref):
    total = got_ref[0, 8:24, :].astype(f32)
    for j in range(1, 16):
        total = total + got_ref[j, 8:24, :].astype(f32)
    total = total.astype(bf16)
    for j in range(16):
        send_ref[j] = total


def place_output(got_ref, out_ref, wide_ref):
    for slot, d in enumerate(ORDER_SLABS):
        for r in range(4):
            wide_ref[pl.ds(4 * d + r, 8, stride=64), :] = got_ref[slot, 0:8, LANES * r : LANES * r + LANES].astype(f32)
    out_ref[...] = wide_ref[...].astype(bf16)


def sum_samples(strided_scale, conv_scale, got_ref, strided_ref, send_ref):
    total = got_ref[0].astype(f32)
    for j in range(1, 16):
        total = total + got_ref[j].astype(f32)
    strided_ref[...] = total[:8] * strided_scale
    conv = (total[8:] * conv_scale).astype(bf16)
    for j in range(16):
        send_ref[j] = conv


def place_conv(got_ref, out_ref):
    for slot, j in enumerate(ORDER_OUT):
        rows, side = 8 * (j // 2), 512 * (j % 2)
        width = min(512, 864 - side)
        out_ref[rows : rows + 8, side : side + width] = got_ref[slot, :, :width].astype(f32)


def shards(volume, conv_weight, strided_weight, cotangent):
    depth = volume.shape[2]
    n_space, n_dp = lax.axis_size("space"), lax.axis_size("dp")
    cells = n_dp * depth * n_space * volume.shape[3] * volume.shape[4]
    between_chips = [pair for i in range(1, n_space - 1, 2) for pair in ((i, i + 1), (i + 1, i))]
    in_chip = [pair for i in range(0, n_space, 2) for pair in ((i, i + 1), (i + 1, i))]

    def shape(dims, dtype):
        return jax.ShapeDtypeStruct(dims, dtype)

    plane = shape((8, 64, LANES), bf16)
    send = call(
        send_first, shape((16, 8, 1024), bf16),
        [
            pltpu.VMEM((512, LANES), bf16),
            pltpu.VMEM((8, 512), bf16),
            pltpu.VMEM((512, LANES), f32),
            pltpu.SemaphoreType.DMA((2,)),
        ],
        0, 400_000,
        *(pltpu.with_memory_space_constraint(x, pltpu.HBM) for x in (cotangent.reshape(512, LANES), strided_weight)),
        space=pltpu.HBM,
    )
    got = lax.all_to_all(send, "space", 0, 0, tiled=True, axis_index_groups=[ORDER_IN])
    cells_in, _ = lax.optimization_barrier((volume, send))
    across_vol, inside_vol = call(
        split_columns, (plane, plane),
        [pltpu.VMEM((2, 512, LANES), f32), pltpu.VMEM((2, 8, 64, LANES), bf16)], 4_000_000_000, 2_000_000,
        cells_in.reshape(512, 256),
    )
    across_got = lax.ppermute(across_vol, "space", between_chips)
    inside_got = lax.ppermute(inside_vol, "space", in_chip)
    grad_plane = shape((8, LANES, LANES), bf16)
    scratch = [pltpu.VMEM((3, 10, LANES, LANES), bf16), pltpu.VMEM((256, 512), f32), pltpu.VMEM((256, 512), bf16)]
    inside_grad, conv_terms, out_terms, strided_terms = call(
        inside,
        (grad_plane, shape((LANES, 9 * LANES), f32), shape((LANES, 512), f32), shape((LANES, 256), f32)),
        scratch, 3_000_000_000, 2_000_000,
        across_vol, inside_vol, inside_got, got, conv_weight,
    )
    send, across_grad = call(
        across, (shape((16, 24, 512), bf16), grad_plane),
        scratch + [pltpu.VMEM((LANES, 9 * LANES), f32)], 3_000_000_000, 3_000_000,
        across_got, across_vol, inside_vol, got, conv_weight, conv_terms, out_terms, strided_terms,
    )
    got = lax.all_to_all(send, "space", 0, 0, tiled=True, axis_index_groups=[ORDER_SLABS])
    own_terms, across_terms, inside_terms = call(
        back, (shape((2, 8, 64, LANES), f32), plane, plane),
        [pltpu.VMEM((2, 10, 256, LANES), bf16), pltpu.VMEM((2, 8, 64, LANES), bf16)],
        3_000_000_000, 3_000_000,
        across_grad, inside_grad, conv_weight,
    )
    got, own_terms, across_terms, inside_terms = lax.optimization_barrier(
        (got, own_terms, across_terms, inside_terms)
    )
    across_got = lax.ppermute(across_terms, "space", between_chips)
    inside_got = lax.ppermute(inside_terms, "space", in_chip)
    send = call(sum_space, shape((16, 16, 512), bf16), [], 0, 600_000, got)
    output = call(place_output, shape((512, LANES), bf16), [pltpu.VMEM((512, LANES), f32)], 0, 600_000, got)
    got = lax.all_to_all(send, "dp", 0, 0, tiled=True, axis_index_groups=[ORDER_SAMPLES])
    strided_grad, send = call(
        lambda *refs: sum_samples(1.0 / math.sqrt(cells / 8), 1.0 / math.sqrt(cells), *refs),
        (shape((8, 512), f32), shape((16, 8, 512), bf16)), [], 0, 600_000, got,
    )
    got = lax.all_to_all(send, "space", 0, 0, tiled=True, axis_index_groups=[ORDER_OUT])
    vol_grad = call(
        finish, shape((512, 256), bf16),
        [
            pltpu.VMEM((2, 8, 64, LANES), f32),
            pltpu.VMEM((512, 256), bf16),
            pltpu.VMEM((2, 512, LANES), f32),
        ],
        1_000_000_000, 2_000_000,
        own_terms, across_got, inside_got,
    )
    conv_grad = call(place_conv, shape((64, 864), f32), [], 0, 300_000, got)
    return output.reshape(cotangent.shape), vol_grad.reshape(volume.shape), conv_grad, strided_grad


def solution(mesh):
    return jax.shard_map(
        shards,
        mesh=mesh,
        in_specs=(
            P("dp", None, "space", None, None),
            P(),
            P("space", None),
            P("dp", "space", None, None, None),
        ),
        out_specs=(
            P("dp", "space", None, None, None),
            P("dp", None, "space", None, None),
            P(),
            P("space", None),
        ),
        check_vma=False,
    )
```

```python
import functools
import math

import jax
import jax.numpy as jnp
from jax import lax
from jax.experimental import pallas as pl
from jax.experimental.pallas import tpu as pltpu
from jax.sharding import PartitionSpec as P

root_two_pi = 0.7978845608028654
bf16 = jnp.bfloat16
f32 = jnp.float32
LANES = 128


def rank_order(bits, reverse):
    order = [sum(((rank >> k) & 1) << bit for k, bit in enumerate(bits)) for rank in range(16)]
    return order[::-1] if reverse else order


ORDER_IN = rank_order((1, 2, 3, 0), True)
ORDER_SLABS = rank_order((1, 2, 3, 0), False)
ORDER_SAMPLES = rank_order((3, 0, 1, 2), True)
ORDER_OUT = rank_order((1, 2, 3, 0), True)
VMEM_LIMIT = 16 * 1024 * 1024


def call(kernel, outs, scratch, flops, moved, *args, space=pltpu.VMEM):
    whole = pl.BlockSpec(memory_space=pltpu.VMEM)
    return pl.pallas_call(
        kernel,
        out_shape=outs,
        in_specs=[pl.BlockSpec(memory_space=space)] * len(args),
        out_specs=jax.tree.map(lambda _: whole, outs),
        scratch_shapes=scratch,
        compiler_params=pltpu.CompilerParams(vmem_limit_bytes=VMEM_LIMIT),
        cost_estimate=pl.CostEstimate(flops=flops, bytes_accessed=moved, transcendentals=0),
    )(*args)


def column_split(transposed=False):
    size = 2 * LANES
    source = lax.broadcasted_iota(jnp.int32, (size, size), 1 if transposed else 0)
    place = lax.broadcasted_iota(jnp.int32, (size, size), 0 if transposed else 1)
    hit = source == 2 * (place & (LANES - 1)) + (place >> 7)
    return jnp.where(hit, 1.0, 0.0).astype(bf16)


def shifted(even, odd):
    lane = lax.broadcasted_iota(jnp.int32, even.shape, 1)
    odd_before = jnp.where(lane == 0, 0.0, pltpu.roll(odd, 1, 1))
    even_after = jnp.where(lane == LANES - 1, 0.0, pltpu.roll(even, LANES - 1, 1))
    return [odd_before.astype(bf16), even.astype(bf16), odd.astype(bf16), even_after.astype(bf16)]


def core_index():
    return lax.rem(lax.axis_index("space"), 2)


def send_first(cot_hbm, weight_hbm, out_ref, cot_ref, weight_ref, wide_ref, sems):
    copies = [
        pltpu.make_async_copy(source, target, sems.at[i])
        for i, (source, target) in enumerate(((cot_hbm, cot_ref), (weight_hbm, weight_ref)))
    ]
    for copy in copies:
        copy.start()
    for copy in copies:
        copy.wait()
    wide_ref[...] = cot_ref[...].astype(f32)
    weights = weight_ref[...]
    for slot, d in enumerate(ORDER_IN):
        rows = [wide_ref[pl.ds(4 * d + r, 8, stride=64), :] for r in range(4)]
        out_ref[slot, :, 0:512] = jnp.concatenate(rows, axis=1).astype(bf16)
        out_ref[slot, :, 512:1024] = weights


def split_columns(own_ref, across_ref, inside_ref, flat_ref, planes_ref):
    columns = jnp.dot(own_ref[...], column_split(), preferred_element_type=f32)
    for e in range(2):
        flat_ref[e] = columns[:, LANES * e : LANES * e + LANES]
    for z in range(2):
        for r in range(8):
            for e in range(2):
                cells = flat_ref[e, pl.ds(8 * z + r, 32, stride=16), :]
                planes_ref[z, r, 32 * e : 32 * e + 32, :] = cells.astype(bf16)
    core = core_index()
    across_ref[...] = planes_ref[core]
    inside_ref[...] = planes_ref[1 - core]


def tap_weights(weight_ref):
    mid = weight_ref.shape[0]
    lane = lax.broadcasted_iota(jnp.int32, (mid, LANES), 1)
    tiles = [weight_ref[:, LANES * t : LANES * (t + 1)].astype(f32) for t in range(6)]
    tail = weight_ref[:, 768:864].astype(f32)
    tiles.append(jnp.concatenate([tail, jnp.zeros((mid, 32), f32)], axis=1))
    halves = [[], []]
    for ab in range(9):
        first, inset = divmod(96 * ab, LANES)
        rolled = tiles[first] if inset == 0 else pltpu.roll(tiles[first], LANES - inset, 1)
        if inset > 32:
            after = pltpu.roll(tiles[first + 1], LANES - inset, 1)
            rolled = jnp.where(lane < LANES - inset, rolled, after)
        own = jnp.where(lane < 96, rolled, 0.0)
        halves[0].append(own.astype(bf16))
        halves[1].append(pltpu.roll(own, 32, 1).astype(bf16))
    return jnp.concatenate([jnp.concatenate(half, axis=1) for half in halves], axis=0)


def fill_taps(taps_ref, planes):
    size = taps_ref.shape[2] // 4
    zero = jnp.zeros(taps_ref.shape[2:], bf16)
    for plane, source in planes:
        taps_ref[plane, 0] = zero
        taps_ref[plane, 9] = zero
        for r in range(8):
            cells = source[r].astype(f32)
            for v, piece in enumerate(shifted(cells[:size], cells[size:])):
                taps_ref[plane, 1 + r, size * v : size * v + size, :] = piece


def surroundings(taps_ref, planes, pair):
    return jnp.concatenate(
        [
            jnp.concatenate([taps_ref[plane, 2 * pair + b], taps_ref[plane, 2 * pair + 1 + b]], axis=1)
            for plane in planes
            for b in range(3)
        ],
        axis=0,
    )


def one_plane(preactivation, got_ref, taps_ref, grad_ref, block_ref, grad_plane_ref, conv_ref, z):
    for pair in range(4):
        around = surroundings(taps_ref, range(3), pair)
        pre = preactivation(pair, around)
        square = pre * pre
        inner = root_two_pi * pre * (1.0 + 0.044715 * square)
        hyper = jnp.tanh(inner)
        half = 0.5 * (1.0 + hyper)
        hidden = (pre * half).astype(bf16)
        slope = half + 0.5 * pre * (1.0 - hyper * hyper) * (root_two_pi + (3.0 * 0.044715 * root_two_pi) * square)
        halves = []
        for side in range(2):
            rows = slice(128 * side, 128 * side + 128)
            columns = slice(LANES * pair, LANES * pair + LANES)
            lanes = slice(LANES * side, LANES * side + LANES)
            block_ref[rows, columns] = hidden[:, lanes]
            halves.append((grad_ref[rows, columns] * slope[:, lanes]).astype(bf16))
            grad_plane_ref[2 * pair + side] = halves[side]
        part = lax.dot_general(
            jnp.concatenate(halves, axis=1), around, (((1,), (1,)), ((), ())), preferred_element_type=f32
        )
        if pair == 0:
            conv_ref[...] = part
        else:
            conv_ref[...] += part
    blocks = block_ref[...]
    cot = got_ref[:, :, 0:512].reshape(128, 512)
    filters = got_ref[:, :, pl.ds(pl.multiple_of(512 + 256 * z, 256), 256)].reshape(128, 256)
    out = jnp.dot(filters, blocks, preferred_element_type=f32)
    strided = lax.dot_general(cot, blocks, (((1,), (1,)), ((), ())), preferred_element_type=f32)
    return out, strided


def inside(across_own, inside_own, inside_got, got_ref, weight_ref,
           grad_plane_ref, conv_ref, out_ref, strided_ref, across_grad_ref, across_pre_ref,
           taps_ref, grad_ref, block_ref):
    core = core_index()
    fill_taps(taps_ref, ((2 * core, across_own), (1, inside_own), (2 - 2 * core, inside_got)))
    cot = got_ref[:, :, 0:512].reshape(128, 512)
    for z, ref in ((1 - core, grad_ref), (core, across_grad_ref)):
        filters = got_ref[:, :, pl.ds(pl.multiple_of(512 + 256 * z, 256), 256)].reshape(128, 256)
        ref[...] = jnp.dot(filters.astype(f32).T.astype(bf16), cot, preferred_element_type=f32)
    weights = tap_weights(weight_ref)
    out, strided = one_plane(
        lambda pair, around: jnp.dot(weights, around, preferred_element_type=f32),
        got_ref, taps_ref, grad_ref, block_ref, grad_plane_ref, conv_ref, 1 - core,
    )
    out_ref[...] = out
    strided_ref[...] = strided
    weights = jnp.where(core == 0, weights[:, 384:], weights[:, :768])
    for pair in range(4):
        around = surroundings(taps_ref, (core, core + 1), pair)
        across_pre_ref[pair] = jnp.dot(weights, around, preferred_element_type=f32)


def across(across_got, across_own, inside_own, got_ref, weight_ref, conv_in, out_in, strided_in, grad_ref, pre_ref,
           send_ref, grad_plane_ref, taps_ref, block_ref, conv_ref):
    core = core_index()
    fill_taps(taps_ref, ((2 * core, across_got), (1, across_own), (2 - 2 * core, inside_own)))
    weights = tap_weights(weight_ref)
    weights = jnp.where(core == 0, weights[:, :384], weights[:, 768:])

    def preactivation(pair, around):
        edge = surroundings(taps_ref, (2 * core,), pair)
        return pre_ref[pair] + jnp.dot(weights, edge, preferred_element_type=f32)

    out, strided = one_plane(
        preactivation, got_ref, taps_ref, grad_ref, block_ref, grad_plane_ref, conv_ref, core
    )
    out = out + out_in[...]
    other = strided_in[...]
    strided = jnp.concatenate(
        [jnp.where(core == 0, strided, other), jnp.where(core == 0, other, strided)], axis=1
    )
    lane = lax.broadcasted_iota(jnp.int32, (64, LANES), 1)
    tiles = [jnp.zeros((64, LANES), f32)] * 8
    for ab in range(9):
        lanes = pl.ds(LANES * ab, LANES)
        even = conv_ref[0:64, lanes] + conv_in[0:64, lanes]
        odd = conv_ref[64:128, lanes] + conv_in[64:128, lanes]
        conv = even + pltpu.roll(odd, 96, 1)
        first, inset = divmod(96 * ab, LANES)
        moved = conv if inset == 0 else pltpu.roll(conv, inset, 1)
        tiles[first] = jnp.where((lane >= inset) & (lane < inset + 96), moved, tiles[first])
        if inset > 32:
            tiles[first + 1] = jnp.where(lane < inset - 32, moved, tiles[first + 1])
    conv = jnp.concatenate(tiles, axis=1)
    for slot, j in enumerate(ORDER_SLABS):
        rows, group, side = 8 * ORDER_IN.index(j), 8 * (j // 2), 512 * (j % 2)
        piece = jnp.concatenate(
            [out[rows : rows + 8], strided[rows : rows + 8], conv[group : group + 8, side : side + 512]], axis=0
        )
        send_ref[slot] = piece.astype(bf16)


def back_weights(weight_ref):
    wide = weight_ref[...].astype(f32)
    turned = jnp.concatenate([wide, wide], axis=0).T
    lane = lax.broadcasted_iota(jnp.int32, (32, LANES), 1)
    low = lane < 64
    pieces = []
    for a in range(3):
        for b in range(3):
            at = 32 * 3 * (3 * (2 - a) + 2 - b)
            tap = [turned[at + 32 * e : at + 32 * e + 32] for e in range(3)]
            even = [jnp.where(low, tap[2], tap[1]), jnp.where(low, tap[0], 0.0)]
            odd = [jnp.where(low, 0.0, tap[2]), jnp.where(low, tap[1], tap[0])]
            pieces.append(
                jnp.concatenate([jnp.concatenate(even, axis=1), jnp.concatenate(odd, axis=1)], axis=0).astype(bf16)
            )
    return jnp.concatenate(pieces, axis=1)


def back(across_own, inside_own, weight_ref, own_ref, across_ref, inside_ref, taps_ref, ends_ref):
    core = core_index()
    fill_taps(taps_ref, ((core, across_own), (1 - core, inside_own)))
    weights = back_weights(weight_ref)
    for plane in range(-1, 3):
        sources = [z for z in range(2) if 0 <= z - plane + 1 < 3]
        depth = sources[0] - plane + 1
        columns = weights[:, 768 * depth : 768 * (depth + len(sources))]
        for pair in range(4):
            grad = jnp.dot(columns, surroundings(taps_ref, sources, pair), preferred_element_type=f32)
            for side in range(2):
                part = grad[:, LANES * side : LANES * side + LANES]
                if 0 <= plane < 2:
                    own_ref[plane, 2 * pair + side] = part
                else:
                    ends_ref[(plane + 1) // 3, 2 * pair + side] = part.astype(bf16)
    across_ref[...] = ends_ref[core]
    inside_ref[...] = ends_ref[1 - core]


def finish(own_ref, across_got, inside_got, out_ref, sum_ref, turn_ref, flat_ref):
    core = core_index()
    sum_ref[core] = own_ref[core] + across_got[...].astype(f32)
    sum_ref[1 - core] = own_ref[1 - core] + inside_got[...].astype(f32)
    for row in range(16):
        grad = sum_ref[row // 8, row % 8].astype(bf16)
        turn_ref[32 * row : 32 * row + 32, :] = jnp.concatenate([grad[:32], grad[32:]], axis=1)
    columns = jnp.dot(turn_ref[...], column_split(True), preferred_element_type=f32)
    for row in range(16):
        for side in range(2):
            flat_ref[side, pl.ds(row, 32, stride=16), :] = columns[
                32 * row : 32 * row + 32, LANES * side : LANES * side + LANES
            ]
    for side in range(2):
        out_ref[:, LANES * side : LANES * side + LANES] = flat_ref[side].astype(bf16)


def sum_space(got_ref, send_ref):
    total = summed(got_ref, slice(8, 24)).astype(bf16)
    for j in range(16):
        send_ref[j] = total


def place_output(got_ref, out_ref, wide_ref):
    for slot, d in enumerate(ORDER_SLABS):
        for r in range(4):
            wide_ref[pl.ds(4 * d + r, 8, stride=64), :] = got_ref[slot, 0:8, LANES * r : LANES * r + LANES].astype(f32)
    out_ref[...] = wide_ref[...].astype(bf16)


def summed(got_ref, rows):
    total = got_ref[0, rows, :].astype(f32)
    for j in range(1, 16):
        total = total + got_ref[j, rows, :].astype(f32)
    return total


def sum_conv(scale, got_ref, send_ref):
    conv = (summed(got_ref, slice(8, 16)) * scale).astype(bf16)
    for j in range(16):
        send_ref[j] = conv


def sum_strided(scale, got_ref, strided_ref):
    strided_ref[...] = summed(got_ref, slice(0, 8)) * scale


def place_conv(got_ref, out_ref):
    for slot, j in enumerate(ORDER_OUT):
        rows, side = 8 * (j // 2), 512 * (j % 2)
        width = min(512, 864 - side)
        out_ref[rows : rows + 8, side : side + width] = got_ref[slot, :, :width].astype(f32)


def shards(volume, conv_weight, strided_weight, cotangent):
    depth = volume.shape[2]
    n_space, n_dp = lax.axis_size("space"), lax.axis_size("dp")
    cells = n_dp * depth * n_space * volume.shape[3] * volume.shape[4]
    between_chips = [pair for i in range(1, n_space - 1, 2) for pair in ((i, i + 1), (i + 1, i))]
    in_chip = [pair for i in range(0, n_space, 2) for pair in ((i, i + 1), (i + 1, i))]

    def shape(dims, dtype):
        return jax.ShapeDtypeStruct(dims, dtype)

    def buffer(*dims):
        return pltpu.VMEM(dims, bf16)

    plane = shape((8, 64, LANES), bf16)
    send = call(
        send_first, buffer(16, 8, 1024),
        [
            pltpu.VMEM((512, LANES), bf16),
            pltpu.VMEM((8, 512), bf16),
            pltpu.VMEM((512, LANES), f32),
            pltpu.SemaphoreType.DMA((2,)),
        ],
        0, 400_000,
        *(pltpu.with_memory_space_constraint(x, pltpu.HBM) for x in (cotangent.reshape(512, LANES), strided_weight)),
        space=pltpu.HBM,
    )
    got = lax.all_to_all(send, "space", 0, 0, tiled=True, axis_index_groups=[ORDER_IN])
    cells_in, _ = lax.optimization_barrier((volume, send))
    across_vol, inside_vol = call(
        split_columns, (plane, plane),
        [pltpu.VMEM((2, 512, LANES), f32), pltpu.VMEM((2, 8, 64, LANES), bf16)], 4_000_000_000, 2_000_000,
        cells_in.reshape(512, 256),
    )
    across_got = lax.ppermute(across_vol, "space", between_chips)
    inside_got = lax.ppermute(inside_vol, "space", in_chip)
    grad_plane = shape((8, LANES, LANES), bf16)
    taps = pltpu.VMEM((3, 10, LANES, LANES), bf16)
    blocks = pltpu.VMEM((256, 512), bf16)
    conv_part = (LANES, 9 * LANES)
    inside_grad, *terms = call(
        inside,
        (
            grad_plane, shape(conv_part, f32), shape((LANES, 512), f32), shape((LANES, 256), f32),
            shape((256, 512), f32), shape((4, LANES, 256), f32),
        ),
        [taps, pltpu.VMEM((256, 512), f32), blocks], 3_000_000_000, 2_000_000,
        across_vol, inside_vol, inside_got, got, conv_weight,
    )
    send, across_grad = call(
        across, (buffer(16, 24, 512), grad_plane),
        [taps, blocks, pltpu.VMEM(conv_part, f32)], 3_000_000_000, 3_000_000,
        across_got, across_vol, inside_vol, got, conv_weight, *terms,
    )
    got = lax.all_to_all(send, "space", 0, 0, tiled=True, axis_index_groups=[ORDER_SLABS])
    own_terms, across_terms, inside_terms = call(
        back, (shape((2, 8, 64, LANES), f32), plane, plane),
        [pltpu.VMEM((2, 10, 256, LANES), bf16), pltpu.VMEM((2, 8, 64, LANES), bf16)],
        3_000_000_000, 3_000_000,
        across_grad, inside_grad, conv_weight,
    )
    got, own_terms, across_terms, inside_terms = lax.optimization_barrier(
        (got, own_terms, across_terms, inside_terms)
    )
    across_got = lax.ppermute(across_terms, "space", between_chips)
    inside_got = lax.ppermute(inside_terms, "space", in_chip)
    send = call(sum_space, buffer(16, 16, 512), [], 0, 600_000, got)
    output = call(place_output, shape((512, LANES), bf16), [pltpu.VMEM((512, LANES), f32)], 0, 600_000, got)
    got = lax.all_to_all(send, "dp", 0, 0, tiled=True, axis_index_groups=[ORDER_SAMPLES])
    send = call(
        functools.partial(sum_conv, 1.0 / math.sqrt(cells)), buffer(16, 8, 512), [], 0, 300_000, got,
    )
    strided_grad = call(
        functools.partial(sum_strided, 1.0 / math.sqrt(cells / 8)), shape((8, 512), f32), [], 0, 300_000, got,
    )
    got = lax.all_to_all(send, "space", 0, 0, tiled=True, axis_index_groups=[ORDER_OUT])
    vol_grad = call(
        finish, shape((512, 256), bf16),
        [
            pltpu.VMEM((2, 8, 64, LANES), f32),
            pltpu.VMEM((512, 256), bf16),
            pltpu.VMEM((2, 512, LANES), f32),
        ],
        1_000_000_000, 2_000_000,
        own_terms, across_got, inside_got,
    )
    conv_grad = call(place_conv, shape((64, 864), f32), [], 0, 300_000, got)
    return output.reshape(cotangent.shape), vol_grad.reshape(volume.shape), conv_grad, strided_grad


def solution(mesh):
    return jax.shard_map(
        shards,
        mesh=mesh,
        in_specs=(
            P("dp", None, "space", None, None),
            P(),
            P("space", None),
            P("dp", "space", None, None, None),
        ),
        out_specs=(
            P("dp", "space", None, None, None),
            P("dp", None, "space", None, None),
            P(),
            P("space", None),
        ),
        check_vma=False,
    )
```

```python
import functools
import math

import jax
import jax.numpy as jnp
from jax import lax
from jax.experimental import pallas as pl
from jax.experimental.pallas import tpu as pltpu
from jax.sharding import PartitionSpec as P

root_two_pi = 0.7978845608028654
bf16 = jnp.bfloat16
f32 = jnp.float32
LANES = 128


def rank_order(bits, reverse):
    order = [sum(((rank >> k) & 1) << bit for k, bit in enumerate(bits)) for rank in range(16)]
    return order[::-1] if reverse else order


ORDER_IN = rank_order((1, 2, 3, 0), True)
ORDER_SLABS = rank_order((1, 2, 3, 0), False)
ORDER_SAMPLES = rank_order((3, 0, 1, 2), True)
ORDER_OUT = rank_order((1, 2, 3, 0), True)
VMEM_LIMIT = 16 * 1024 * 1024


def call(kernel, outs, scratch, flops, moved, *args, space=pltpu.VMEM):
    whole = pl.BlockSpec(memory_space=pltpu.VMEM)
    return pl.pallas_call(
        kernel,
        out_shape=outs,
        in_specs=[pl.BlockSpec(memory_space=space)] * len(args),
        out_specs=jax.tree.map(lambda _: whole, outs),
        scratch_shapes=scratch,
        compiler_params=pltpu.CompilerParams(vmem_limit_bytes=VMEM_LIMIT),
        cost_estimate=pl.CostEstimate(flops=flops, bytes_accessed=moved, transcendentals=0),
    )(*args)


def column_split(transposed=False):
    size = 2 * LANES
    source = lax.broadcasted_iota(jnp.int32, (size, size), 1 if transposed else 0)
    place = lax.broadcasted_iota(jnp.int32, (size, size), 0 if transposed else 1)
    hit = source == 2 * (place & (LANES - 1)) + (place >> 7)
    return jnp.where(hit, 1.0, 0.0).astype(bf16)


def shifted(even, odd):
    lane = lax.broadcasted_iota(jnp.int32, even.shape, 1)
    odd_before = jnp.where(lane == 0, 0.0, pltpu.roll(odd, 1, 1))
    even_after = jnp.where(lane == LANES - 1, 0.0, pltpu.roll(even, LANES - 1, 1))
    return [odd_before.astype(bf16), even.astype(bf16), odd.astype(bf16), even_after.astype(bf16)]


def core_index():
    return lax.rem(lax.axis_index("space"), 2)


def send_first(cot_hbm, weight_hbm, out_ref, cot_ref, weight_ref, wide_ref, sems):
    copies = [
        pltpu.make_async_copy(source, target, sems.at[i])
        for i, (source, target) in enumerate(((cot_hbm, cot_ref), (weight_hbm, weight_ref)))
    ]
    for copy in copies:
        copy.start()
    for copy in copies:
        copy.wait()
    wide_ref[0:512, :] = cot_ref[...].astype(f32)
    weights = weight_ref[...]
    for slot, d in enumerate(ORDER_IN):
        rows = [wide_ref[pl.ds(4 * d + r, 8, stride=64), :] for r in range(4)]
        out_ref[slot, :, 0:512] = jnp.concatenate(rows, axis=1).astype(bf16)
        out_ref[slot, :, 512:1024] = weights


def split_columns(own_ref, across_ref, inside_ref, flat_ref, planes_ref):
    columns = jnp.dot(own_ref[...], column_split(), preferred_element_type=f32)
    for e in range(2):
        flat_ref[e, 0:512, :] = columns[:, LANES * e : LANES * e + LANES]
    for z in range(2):
        for r in range(8):
            for e in range(2):
                cells = flat_ref[e, pl.ds(8 * z + r, 32, stride=16), :]
                planes_ref[z, r, 32 * e : 32 * e + 32, :] = cells.astype(bf16)
    core = core_index()
    across_ref[...] = planes_ref[core]
    inside_ref[...] = planes_ref[1 - core]


def tap_weights(weight_ref):
    mid = weight_ref.shape[0]
    lane = lax.broadcasted_iota(jnp.int32, (mid, LANES), 1)
    tiles = [weight_ref[:, LANES * t : LANES * (t + 1)].astype(f32) for t in range(6)]
    tail = weight_ref[:, 768:864].astype(f32)
    tiles.append(jnp.concatenate([tail, jnp.zeros((mid, 32), f32)], axis=1))
    halves = [[], []]
    for ab in range(9):
        first, inset = divmod(96 * ab, LANES)
        rolled = tiles[first] if inset == 0 else pltpu.roll(tiles[first], LANES - inset, 1)
        if inset > 32:
            after = pltpu.roll(tiles[first + 1], LANES - inset, 1)
            rolled = jnp.where(lane < LANES - inset, rolled, after)
        own = jnp.where(lane < 96, rolled, 0.0)
        halves[0].append(own.astype(bf16))
        halves[1].append(pltpu.roll(own, 32, 1).astype(bf16))
    return jnp.concatenate([jnp.concatenate(half, axis=1) for half in halves], axis=0)


def fill_taps(taps_ref, planes):
    size = taps_ref.shape[2] // 4
    zero = jnp.zeros(taps_ref.shape[2:], bf16)
    for plane, source in planes:
        taps_ref[plane, 0] = zero
        taps_ref[plane, 9] = zero
        for r in range(8):
            cells = source[r].astype(f32)
            for v, piece in enumerate(shifted(cells[:size], cells[size:])):
                taps_ref[plane, 1 + r, size * v : size * v + size, :] = piece


def surroundings(taps_ref, planes, pair):
    return jnp.concatenate(
        [
            jnp.concatenate([taps_ref[plane, 2 * pair + b], taps_ref[plane, 2 * pair + 1 + b]], axis=1)
            for plane in planes
            for b in range(3)
        ],
        axis=0,
    )


def one_plane(preactivation, got_ref, taps_ref, grad_ref, block_ref, grad_plane_ref, conv_ref, z):
    for pair in range(4):
        around = surroundings(taps_ref, range(3), pair)
        pre = preactivation(pair, around)
        square = pre * pre
        inner = root_two_pi * pre * (1.0 + 0.044715 * square)
        hyper = jnp.tanh(inner)
        half = 0.5 * (1.0 + hyper)
        hidden = (pre * half).astype(bf16)
        slope = half + 0.5 * pre * (1.0 - hyper * hyper) * (root_two_pi + (3.0 * 0.044715 * root_two_pi) * square)
        halves = []
        for side in range(2):
            rows = slice(128 * side, 128 * side + 128)
            columns = slice(LANES * pair, LANES * pair + LANES)
            lanes = slice(LANES * side, LANES * side + LANES)
            block_ref[rows, columns] = hidden[:, lanes]
            halves.append((grad_ref[rows, columns] * slope[:, lanes]).astype(bf16))
            grad_plane_ref[2 * pair + side] = halves[side]
        part = lax.dot_general(
            jnp.concatenate(halves, axis=1), around, (((1,), (1,)), ((), ())), preferred_element_type=f32
        )
        if pair == 0:
            conv_ref[...] = part
        else:
            conv_ref[...] += part
    blocks = block_ref[...]
    cot = got_ref[:, :, 0:512].reshape(128, 512)
    filters = got_ref[:, :, pl.ds(pl.multiple_of(512 + 256 * z, 256), 256)].reshape(128, 256)
    out = jnp.dot(filters, blocks, preferred_element_type=f32)
    strided = lax.dot_general(cot, blocks, (((1,), (1,)), ((), ())), preferred_element_type=f32)
    return out, strided


def inside(across_own, inside_own, inside_got, got_ref, weight_ref,
           grad_plane_ref, conv_ref, out_ref, strided_ref, across_grad_ref, across_pre_ref,
           taps_ref, grad_ref, block_ref):
    core = core_index()
    fill_taps(taps_ref, ((2 * core, across_own), (1, inside_own), (2 - 2 * core, inside_got)))
    cot = got_ref[:, :, 0:512].reshape(128, 512)
    for z, ref in ((1 - core, grad_ref), (core, across_grad_ref)):
        filters = got_ref[:, :, pl.ds(pl.multiple_of(512 + 256 * z, 256), 256)].reshape(128, 256)
        ref[...] = jnp.dot(filters.astype(f32).T.astype(bf16), cot, preferred_element_type=f32)
    weights = tap_weights(weight_ref)
    out, strided = one_plane(
        lambda pair, around: jnp.dot(weights, around, preferred_element_type=f32),
        got_ref, taps_ref, grad_ref, block_ref, grad_plane_ref, conv_ref, 1 - core,
    )
    out_ref[...] = out
    strided_ref[...] = strided
    weights = jnp.where(core == 0, weights[:, 384:], weights[:, :768])
    for pair in range(4):
        around = surroundings(taps_ref, (core, core + 1), pair)
        across_pre_ref[pair] = jnp.dot(weights, around, preferred_element_type=f32)


def across(across_got, across_own, inside_own, got_ref, weight_ref, conv_in, out_in, strided_in, grad_ref, pre_ref,
           send_ref, grad_plane_ref, taps_ref, block_ref, conv_ref):
    core = core_index()
    fill_taps(taps_ref, ((2 * core, across_got), (1, across_own), (2 - 2 * core, inside_own)))
    weights = tap_weights(weight_ref)
    weights = jnp.where(core == 0, weights[:, :384], weights[:, 768:])

    def preactivation(pair, around):
        edge = surroundings(taps_ref, (2 * core,), pair)
        return pre_ref[pair] + jnp.dot(weights, edge, preferred_element_type=f32)

    out, strided = one_plane(
        preactivation, got_ref, taps_ref, grad_ref, block_ref, grad_plane_ref, conv_ref, core
    )
    out = out + out_in[...]
    other = strided_in[...]
    strided = jnp.concatenate(
        [jnp.where(core == 0, strided, other), jnp.where(core == 0, other, strided)], axis=1
    )
    lane = lax.broadcasted_iota(jnp.int32, (64, LANES), 1)
    tiles = [jnp.zeros((64, LANES), f32)] * 8
    for ab in range(9):
        lanes = pl.ds(LANES * ab, LANES)
        even = conv_ref[0:64, lanes] + conv_in[0:64, lanes]
        odd = conv_ref[64:128, lanes] + conv_in[64:128, lanes]
        conv = even + pltpu.roll(odd, 96, 1)
        first, inset = divmod(96 * ab, LANES)
        moved = conv if inset == 0 else pltpu.roll(conv, inset, 1)
        tiles[first] = jnp.where((lane >= inset) & (lane < inset + 96), moved, tiles[first])
        if inset > 32:
            tiles[first + 1] = jnp.where(lane < inset - 32, moved, tiles[first + 1])
    conv = jnp.concatenate(tiles, axis=1)
    for slot, j in enumerate(ORDER_SLABS):
        rows, group, side = 8 * ORDER_IN.index(j), 8 * (j // 2), 512 * (j % 2)
        piece = jnp.concatenate(
            [out[rows : rows + 8], strided[rows : rows + 8], conv[group : group + 8, side : side + 512]], axis=0
        )
        send_ref[slot] = piece.astype(bf16)


def back_weights(weight_ref):
    wide = weight_ref[...].astype(f32)
    turned = jnp.concatenate([wide, wide], axis=0).T
    lane = lax.broadcasted_iota(jnp.int32, (32, LANES), 1)
    low = lane < 64
    pieces = []
    for a in range(3):
        for b in range(3):
            at = 32 * 3 * (3 * (2 - a) + 2 - b)
            tap = [turned[at + 32 * e : at + 32 * e + 32] for e in range(3)]
            even = [jnp.where(low, tap[2], tap[1]), jnp.where(low, tap[0], 0.0)]
            odd = [jnp.where(low, 0.0, tap[2]), jnp.where(low, tap[1], tap[0])]
            pieces.append(
                jnp.concatenate([jnp.concatenate(even, axis=1), jnp.concatenate(odd, axis=1)], axis=0).astype(bf16)
            )
    return jnp.concatenate(pieces, axis=1)


def back(across_own, inside_own, weight_ref, own_ref, across_ref, inside_ref, taps_ref, ends_ref):
    core = core_index()
    fill_taps(taps_ref, ((core, across_own), (1 - core, inside_own)))
    weights = back_weights(weight_ref)
    for plane in range(-1, 3):
        sources = [z for z in range(2) if 0 <= z - plane + 1 < 3]
        depth = sources[0] - plane + 1
        columns = weights[:, 768 * depth : 768 * (depth + len(sources))]
        for pair in range(4):
            grad = jnp.dot(columns, surroundings(taps_ref, sources, pair), preferred_element_type=f32)
            for side in range(2):
                part = grad[:, LANES * side : LANES * side + LANES]
                if 0 <= plane < 2:
                    own_ref[plane, 2 * pair + side] = part
                else:
                    ends_ref[(plane + 1) // 3, 2 * pair + side] = part.astype(bf16)
    across_ref[...] = ends_ref[core]
    inside_ref[...] = ends_ref[1 - core]


def finish(own_ref, across_got, inside_got, out_ref, sum_ref, turn_ref, flat_ref):
    core = core_index()
    sum_ref[core] = own_ref[core] + across_got[...].astype(f32)
    sum_ref[1 - core] = own_ref[1 - core] + inside_got[...].astype(f32)
    for row in range(16):
        grad = sum_ref[row // 8, row % 8].astype(bf16)
        turn_ref[32 * row : 32 * row + 32, :] = jnp.concatenate([grad[:32], grad[32:]], axis=1)
    columns = jnp.dot(turn_ref[...], column_split(True), preferred_element_type=f32)
    for row in range(16):
        for side in range(2):
            flat_ref[side, pl.ds(row, 32, stride=16), :] = columns[
                32 * row : 32 * row + 32, LANES * side : LANES * side + LANES
            ]
    for side in range(2):
        out_ref[:, LANES * side : LANES * side + LANES] = flat_ref[side, 0:512, :].astype(bf16)


def sum_space(got_ref, send_ref):
    total = summed(got_ref, slice(8, 24)).astype(bf16)
    for j in range(16):
        send_ref[j] = total


def place_output(got_ref, out_ref, wide_ref):
    for slot, d in enumerate(ORDER_SLABS):
        for r in range(4):
            wide_ref[pl.ds(4 * d + r, 8, stride=64), :] = got_ref[slot, 0:8, LANES * r : LANES * r + LANES].astype(f32)
    out_ref[...] = wide_ref[0:512, :].astype(bf16)


def summed(got_ref, rows):
    total = got_ref[0, rows, :].astype(f32)
    for j in range(1, 16):
        total = total + got_ref[j, rows, :].astype(f32)
    return total


def sum_conv(scale, got_ref, send_ref):
    conv = (summed(got_ref, slice(8, 16)) * scale).astype(bf16)
    for j in range(16):
        send_ref[j] = conv


def sum_strided(scale, got_ref, strided_ref):
    strided_ref[...] = summed(got_ref, slice(0, 8)) * scale


def place_conv(got_ref, out_ref):
    for slot, j in enumerate(ORDER_OUT):
        rows, side = 8 * (j // 2), 512 * (j % 2)
        width = min(512, 864 - side)
        out_ref[rows : rows + 8, side : side + width] = got_ref[slot, :, :width].astype(f32)


def shards(volume, conv_weight, strided_weight, cotangent):
    depth = volume.shape[2]
    n_space, n_dp = lax.axis_size("space"), lax.axis_size("dp")
    cells = n_dp * depth * n_space * volume.shape[3] * volume.shape[4]
    between_chips = [pair for i in range(1, n_space - 1, 2) for pair in ((i, i + 1), (i + 1, i))]
    in_chip = [pair for i in range(0, n_space, 2) for pair in ((i, i + 1), (i + 1, i))]

    def shape(dims, dtype):
        return jax.ShapeDtypeStruct(dims, dtype)

    def buffer(*dims):
        return pltpu.VMEM(dims, bf16)

    plane = shape((8, 64, LANES), bf16)
    send = call(
        send_first, buffer(16, 8, 1024),
        [
            pltpu.VMEM((512, LANES), bf16),
            pltpu.VMEM((8, 512), bf16),
            pltpu.VMEM((576, LANES), f32),
            pltpu.SemaphoreType.DMA((2,)),
        ],
        0, 400_000,
        *(pltpu.with_memory_space_constraint(x, pltpu.HBM) for x in (cotangent.reshape(512, LANES), strided_weight)),
        space=pltpu.HBM,
    )
    got = lax.all_to_all(send, "space", 0, 0, tiled=True, axis_index_groups=[ORDER_IN])
    cells_in, _ = lax.optimization_barrier((volume, send))
    across_vol, inside_vol = call(
        split_columns, (plane, plane),
        [pltpu.VMEM((2, 528, LANES), f32), pltpu.VMEM((2, 8, 64, LANES), bf16)], 4_000_000_000, 2_000_000,
        cells_in.reshape(512, 256),
    )
    across_got = lax.ppermute(across_vol, "space", between_chips)
    inside_got = lax.ppermute(inside_vol, "space", in_chip)
    grad_plane = shape((8, LANES, LANES), bf16)
    taps = pltpu.VMEM((3, 10, LANES, LANES), bf16)
    blocks = pltpu.VMEM((256, 512), bf16)
    conv_part = (LANES, 9 * LANES)
    inside_grad, *terms = call(
        inside,
        (
            grad_plane, shape(conv_part, f32), shape((LANES, 512), f32), shape((LANES, 256), f32),
            shape((256, 512), f32), shape((4, LANES, 256), f32),
        ),
        [taps, pltpu.VMEM((256, 512), f32), blocks], 3_000_000_000, 2_000_000,
        across_vol, inside_vol, inside_got, got, conv_weight,
    )
    send, across_grad = call(
        across, (buffer(16, 24, 512), grad_plane),
        [taps, blocks, pltpu.VMEM(conv_part, f32)], 3_000_000_000, 3_000_000,
        across_got, across_vol, inside_vol, got, conv_weight, *terms,
    )
    got = lax.all_to_all(send, "space", 0, 0, tiled=True, axis_index_groups=[ORDER_SLABS])
    own_terms, across_terms, inside_terms = call(
        back, (shape((2, 8, 64, LANES), f32), plane, plane),
        [pltpu.VMEM((2, 10, 256, LANES), bf16), pltpu.VMEM((2, 8, 64, LANES), bf16)],
        3_000_000_000, 3_000_000,
        across_grad, inside_grad, conv_weight,
    )
    got, own_terms, across_terms, inside_terms = lax.optimization_barrier(
        (got, own_terms, across_terms, inside_terms)
    )
    across_got = lax.ppermute(across_terms, "space", between_chips)
    inside_got = lax.ppermute(inside_terms, "space", in_chip)
    send = call(sum_space, buffer(16, 16, 512), [], 0, 600_000, got)
    output = call(place_output, shape((512, LANES), bf16), [pltpu.VMEM((576, LANES), f32)], 0, 600_000, got)
    got = lax.all_to_all(send, "dp", 0, 0, tiled=True, axis_index_groups=[ORDER_SAMPLES])
    send = call(
        functools.partial(sum_conv, 1.0 / math.sqrt(cells)), buffer(16, 8, 512), [], 0, 300_000, got,
    )
    strided_grad = call(
        functools.partial(sum_strided, 1.0 / math.sqrt(cells / 8)), shape((8, 512), f32), [], 0, 300_000, got,
    )
    got = lax.all_to_all(send, "space", 0, 0, tiled=True, axis_index_groups=[ORDER_OUT])
    vol_grad = call(
        finish, shape((512, 256), bf16),
        [
            pltpu.VMEM((2, 8, 64, LANES), f32),
            pltpu.VMEM((512, 256), bf16),
            pltpu.VMEM((2, 528, LANES), f32),
        ],
        1_000_000_000, 2_000_000,
        own_terms, across_got, inside_got,
    )
    conv_grad = call(place_conv, shape((64, 864), f32), [], 0, 300_000, got)
    return output.reshape(cotangent.shape), vol_grad.reshape(volume.shape), conv_grad, strided_grad


def solution(mesh):
    return jax.shard_map(
        shards,
        mesh=mesh,
        in_specs=(
            P("dp", None, "space", None, None),
            P(),
            P("space", None),
            P("dp", "space", None, None, None),
        ),
        out_specs=(
            P("dp", "space", None, None, None),
            P("dp", None, "space", None, None),
            P(),
            P("space", None),
        ),
        check_vma=False,
    )
```

```python
import functools
import math

import jax
import jax.numpy as jnp
from jax import lax
from jax.experimental import pallas as pl
from jax.experimental.pallas import tpu as pltpu
from jax.sharding import PartitionSpec as P

root_two_pi = 0.7978845608028654
bf16 = jnp.bfloat16
f32 = jnp.float32
LANES = 128


def rank_order(bits, reverse):
    order = [sum(((rank >> k) & 1) << bit for k, bit in enumerate(bits)) for rank in range(16)]
    return order[::-1] if reverse else order


ORDER_IN = rank_order((1, 2, 3, 0), True)
ORDER_SLABS = rank_order((1, 2, 3, 0), False)
ORDER_SAMPLES = rank_order((3, 0, 1, 2), True)
ORDER_OUT = rank_order((1, 2, 3, 0), True)
VMEM_LIMIT = 16 * 1024 * 1024


def call(kernel, outs, scratch, flops, moved, *args, space=pltpu.VMEM):
    whole = pl.BlockSpec(memory_space=pltpu.VMEM)
    return pl.pallas_call(
        kernel,
        out_shape=outs,
        in_specs=[pl.BlockSpec(memory_space=space)] * len(args),
        out_specs=jax.tree.map(lambda _: whole, outs),
        scratch_shapes=scratch,
        compiler_params=pltpu.CompilerParams(vmem_limit_bytes=VMEM_LIMIT),
        cost_estimate=pl.CostEstimate(flops=flops, bytes_accessed=moved, transcendentals=0),
    )(*args)


def column_split(transposed=False):
    size = 2 * LANES
    source = lax.broadcasted_iota(jnp.int32, (size, size), 1 if transposed else 0)
    place = lax.broadcasted_iota(jnp.int32, (size, size), 0 if transposed else 1)
    hit = source == 2 * (place & (LANES - 1)) + (place >> 7)
    return jnp.where(hit, 1.0, 0.0).astype(bf16)


def shifted(even, odd):
    lane = lax.broadcasted_iota(jnp.int32, even.shape, 1)
    odd_before = jnp.where(lane == 0, 0.0, pltpu.roll(odd, 1, 1))
    even_after = jnp.where(lane == LANES - 1, 0.0, pltpu.roll(even, LANES - 1, 1))
    return [odd_before.astype(bf16), even.astype(bf16), odd.astype(bf16), even_after.astype(bf16)]


def core_index():
    return lax.rem(lax.axis_index("space"), 2)


def send_first(cot_hbm, weight_hbm, out_ref, cot_ref, weight_ref, wide_ref, sems):
    copies = [
        pltpu.make_async_copy(source, target, sems.at[i])
        for i, (source, target) in enumerate(((cot_hbm, cot_ref), (weight_hbm, weight_ref)))
    ]
    for copy in copies:
        copy.start()
    for copy in copies:
        copy.wait()
    wide_ref[0:512, :] = cot_ref[...].astype(f32)
    weights = weight_ref[...]
    for slot, d in enumerate(ORDER_IN):
        rows = [wide_ref[pl.ds(4 * d + r, 8, stride=64), :] for r in range(4)]
        out_ref[slot, :, 0:512] = jnp.concatenate(rows, axis=1).astype(bf16)
        out_ref[slot, :, 512:1024] = weights


def split_columns(own_ref, across_ref, inside_ref, flat_ref, planes_ref):
    columns = jnp.dot(own_ref[...], column_split(), preferred_element_type=f32)
    for e in range(2):
        flat_ref[e, 0:512, :] = columns[:, LANES * e : LANES * e + LANES]
    for z in range(2):
        for r in range(8):
            for e in range(2):
                cells = flat_ref[e, pl.ds(8 * z + r, 32, stride=16), :]
                planes_ref[z, r, 32 * e : 32 * e + 32, :] = cells.astype(bf16)
    core = core_index()
    across_ref[...] = planes_ref[core]
    inside_ref[...] = planes_ref[1 - core]


def tap_weights(weight_ref):
    mid = weight_ref.shape[0]
    lane = lax.broadcasted_iota(jnp.int32, (mid, LANES), 1)
    tiles = [weight_ref[:, LANES * t : LANES * (t + 1)].astype(f32) for t in range(6)]
    tail = weight_ref[:, 768:864].astype(f32)
    tiles.append(jnp.concatenate([tail, jnp.zeros((mid, 32), f32)], axis=1))
    halves = [[], []]
    for ab in range(9):
        first, inset = divmod(96 * ab, LANES)
        rolled = tiles[first] if inset == 0 else pltpu.roll(tiles[first], LANES - inset, 1)
        if inset > 32:
            after = pltpu.roll(tiles[first + 1], LANES - inset, 1)
            rolled = jnp.where(lane < LANES - inset, rolled, after)
        own = jnp.where(lane < 96, rolled, 0.0)
        halves[0].append(own.astype(bf16))
        halves[1].append(pltpu.roll(own, 32, 1).astype(bf16))
    return jnp.concatenate([jnp.concatenate(half, axis=1) for half in halves], axis=0)


def fill_taps(taps_ref, planes):
    size = taps_ref.shape[2] // 4
    zero = jnp.zeros(taps_ref.shape[2:], bf16)
    for plane, source in planes:
        taps_ref[plane, 0] = zero
        taps_ref[plane, 9] = zero
        for r in range(8):
            cells = source[r].astype(f32)
            for v, piece in enumerate(shifted(cells[:size], cells[size:])):
                taps_ref[plane, 1 + r, size * v : size * v + size, :] = piece


def surroundings(taps_ref, planes, pair):
    return jnp.concatenate(
        [
            jnp.concatenate([taps_ref[plane, 2 * pair + b], taps_ref[plane, 2 * pair + 1 + b]], axis=1)
            for plane in planes
            for b in range(3)
        ],
        axis=0,
    )


def one_plane(preactivation, got_ref, taps_ref, grad_ref, block_ref, grad_plane_ref, conv_ref, z):
    for pair in range(4):
        around = surroundings(taps_ref, range(3), pair)
        pre = preactivation(pair, around)
        square = pre * pre
        inner = root_two_pi * pre * (1.0 + 0.044715 * square)
        hyper = jnp.tanh(inner)
        half = 0.5 * (1.0 + hyper)
        hidden = (pre * half).astype(bf16)
        slope = half + 0.5 * pre * (1.0 - hyper * hyper) * (root_two_pi + (3.0 * 0.044715 * root_two_pi) * square)
        halves = []
        for side in range(2):
            rows = slice(128 * side, 128 * side + 128)
            columns = slice(LANES * pair, LANES * pair + LANES)
            lanes = slice(LANES * side, LANES * side + LANES)
            block_ref[rows, columns] = hidden[:, lanes]
            halves.append((grad_ref[rows, columns] * slope[:, lanes]).astype(bf16))
            grad_plane_ref[2 * pair + side] = halves[side]
        part = lax.dot_general(
            jnp.concatenate(halves, axis=1), around, (((1,), (1,)), ((), ())), preferred_element_type=f32
        )
        if pair == 0:
            conv_ref[...] = part
        else:
            conv_ref[...] += part
    blocks = block_ref[...]
    cot = got_ref[:, :, 0:512].reshape(128, 512)
    filters = got_ref[:, :, pl.ds(pl.multiple_of(512 + 256 * z, 256), 256)].reshape(128, 256)
    out = jnp.dot(filters, blocks, preferred_element_type=f32)
    strided = lax.dot_general(cot, blocks, (((1,), (1,)), ((), ())), preferred_element_type=f32)
    return out, strided


def inside(across_own, inside_own, inside_got, got_ref, weight_ref,
           grad_plane_ref, conv_ref, out_ref, strided_ref, across_grad_ref, across_pre_ref,
           taps_ref, grad_ref, block_ref):
    core = core_index()
    fill_taps(taps_ref, ((2 * core, across_own), (1, inside_own), (2 - 2 * core, inside_got)))
    cot = got_ref[:, :, 0:512].reshape(128, 512)
    for z, ref in ((1 - core, grad_ref), (core, across_grad_ref)):
        filters = got_ref[:, :, pl.ds(pl.multiple_of(512 + 256 * z, 256), 256)].reshape(128, 256)
        ref[...] = jnp.dot(filters.astype(f32).T.astype(bf16), cot, preferred_element_type=f32)
    weights = tap_weights(weight_ref)
    out, strided = one_plane(
        lambda pair, around: jnp.dot(weights, around, preferred_element_type=f32),
        got_ref, taps_ref, grad_ref, block_ref, grad_plane_ref, conv_ref, 1 - core,
    )
    out_ref[...] = out
    strided_ref[...] = strided
    weights = jnp.where(core == 0, weights[:, 384:], weights[:, :768])
    for pair in range(4):
        around = surroundings(taps_ref, (core, core + 1), pair)
        across_pre_ref[pair] = jnp.dot(weights, around, preferred_element_type=f32)


def across(across_got, across_own, inside_own, got_ref, weight_ref, conv_in, out_in, strided_in, grad_ref, pre_ref,
           send_ref, grad_plane_ref, taps_ref, block_ref, conv_ref):
    core = core_index()
    fill_taps(taps_ref, ((2 * core, across_got), (1, across_own), (2 - 2 * core, inside_own)))
    weights = tap_weights(weight_ref)
    weights = jnp.where(core == 0, weights[:, :384], weights[:, 768:])

    def preactivation(pair, around):
        edge = surroundings(taps_ref, (2 * core,), pair)
        return pre_ref[pair] + jnp.dot(weights, edge, preferred_element_type=f32)

    out, strided = one_plane(
        preactivation, got_ref, taps_ref, grad_ref, block_ref, grad_plane_ref, conv_ref, core
    )
    out = out + out_in[...]
    other = strided_in[...]
    strided = jnp.concatenate(
        [jnp.where(core == 0, strided, other), jnp.where(core == 0, other, strided)], axis=1
    )
    lane = lax.broadcasted_iota(jnp.int32, (64, LANES), 1)
    tiles = [jnp.zeros((64, LANES), f32)] * 8
    for ab in range(9):
        lanes = pl.ds(LANES * ab, LANES)
        even = conv_ref[0:64, lanes] + conv_in[0:64, lanes]
        odd = conv_ref[64:128, lanes] + conv_in[64:128, lanes]
        conv = even + pltpu.roll(odd, 96, 1)
        first, inset = divmod(96 * ab, LANES)
        moved = conv if inset == 0 else pltpu.roll(conv, inset, 1)
        tiles[first] = jnp.where((lane >= inset) & (lane < inset + 96), moved, tiles[first])
        if inset > 32:
            tiles[first + 1] = jnp.where(lane < inset - 32, moved, tiles[first + 1])
    conv = jnp.concatenate(tiles, axis=1)
    for slot, j in enumerate(ORDER_SLABS):
        rows, group, side = 8 * ORDER_IN.index(j), 8 * (j // 2), 512 * (j % 2)
        piece = jnp.concatenate(
            [out[rows : rows + 8], strided[rows : rows + 8], conv[group : group + 8, side : side + 512]], axis=0
        )
        send_ref[slot] = piece.astype(bf16)


def back_weights(weight_ref):
    wide = weight_ref[...].astype(f32)
    turned = jnp.concatenate([wide, wide], axis=0).T
    lane = lax.broadcasted_iota(jnp.int32, (32, LANES), 1)
    low = lane < 64
    pieces = []
    for a in range(3):
        for b in range(3):
            at = 32 * 3 * (3 * (2 - a) + 2 - b)
            tap = [turned[at + 32 * e : at + 32 * e + 32] for e in range(3)]
            even = [jnp.where(low, tap[2], tap[1]), jnp.where(low, tap[0], 0.0)]
            odd = [jnp.where(low, 0.0, tap[2]), jnp.where(low, tap[1], tap[0])]
            pieces.append(
                jnp.concatenate([jnp.concatenate(even, axis=1), jnp.concatenate(odd, axis=1)], axis=0).astype(bf16)
            )
    return jnp.concatenate(pieces, axis=1)


def back(across_own, inside_own, weight_ref, own_ref, across_ref, inside_ref, taps_ref, ends_ref):
    core = core_index()
    fill_taps(taps_ref, ((core, across_own), (1 - core, inside_own)))
    weights = back_weights(weight_ref)
    for plane in range(-1, 3):
        sources = [z for z in range(2) if 0 <= z - plane + 1 < 3]
        depth = sources[0] - plane + 1
        columns = weights[:, 768 * depth : 768 * (depth + len(sources))]
        for pair in range(4):
            grad = jnp.dot(columns, surroundings(taps_ref, sources, pair), preferred_element_type=f32)
            for side in range(2):
                part = grad[:, LANES * side : LANES * side + LANES]
                if 0 <= plane < 2:
                    own_ref[plane, 2 * pair + side] = part
                else:
                    ends_ref[(plane + 1) // 3, 2 * pair + side] = part.astype(bf16)
    across_ref[...] = ends_ref[core]
    inside_ref[...] = ends_ref[1 - core]


def finish(scale, got_ref, sums_ref, own_ref, across_got, inside_got, output_ref, strided_ref, out_ref,
           wide_ref, sum_ref, turn_ref, flat_ref):
    place_output(got_ref, output_ref, wide_ref)
    strided_ref[...] = summed(sums_ref, slice(0, 8)) * scale
    core = core_index()
    sum_ref[core] = own_ref[core] + across_got[...].astype(f32)
    sum_ref[1 - core] = own_ref[1 - core] + inside_got[...].astype(f32)
    for row in range(16):
        grad = sum_ref[row // 8, row % 8].astype(bf16)
        turn_ref[32 * row : 32 * row + 32, :] = jnp.concatenate([grad[:32], grad[32:]], axis=1)
    columns = jnp.dot(turn_ref[...], column_split(True), preferred_element_type=f32)
    for row in range(16):
        for side in range(2):
            flat_ref[side, pl.ds(row, 32, stride=16), :] = columns[
                32 * row : 32 * row + 32, LANES * side : LANES * side + LANES
            ]
    for side in range(2):
        out_ref[:, LANES * side : LANES * side + LANES] = flat_ref[side, 0:512, :].astype(bf16)


def sum_space(got_ref, send_ref):
    total = summed(got_ref, slice(8, 24)).astype(bf16)
    for j in range(16):
        send_ref[j] = total


def place_output(got_ref, out_ref, wide_ref):
    for slot, d in enumerate(ORDER_SLABS):
        for r in range(4):
            wide_ref[pl.ds(4 * d + r, 8, stride=64), :] = got_ref[slot, 0:8, LANES * r : LANES * r + LANES].astype(f32)
    out_ref[...] = wide_ref[0:512, :].astype(bf16)


def summed(got_ref, rows):
    total = got_ref[0, rows, :].astype(f32)
    for j in range(1, 16):
        total = total + got_ref[j, rows, :].astype(f32)
    return total


def sum_conv(scale, got_ref, send_ref):
    conv = (summed(got_ref, slice(8, 16)) * scale).astype(bf16)
    for j in range(16):
        send_ref[j] = conv


def place_conv(got_ref, out_ref):
    for slot, j in enumerate(ORDER_OUT):
        rows, side = 8 * (j // 2), 512 * (j % 2)
        width = min(512, 864 - side)
        out_ref[rows : rows + 8, side : side + width] = got_ref[slot, :, :width].astype(f32)


def shards(volume, conv_weight, strided_weight, cotangent):
    depth = volume.shape[2]
    n_space, n_dp = lax.axis_size("space"), lax.axis_size("dp")
    cells = n_dp * depth * n_space * volume.shape[3] * volume.shape[4]
    between_chips = [pair for i in range(1, n_space - 1, 2) for pair in ((i, i + 1), (i + 1, i))]
    in_chip = [pair for i in range(0, n_space, 2) for pair in ((i, i + 1), (i + 1, i))]

    def shape(dims, dtype):
        return jax.ShapeDtypeStruct(dims, dtype)

    def buffer(*dims):
        return pltpu.VMEM(dims, bf16)

    plane = shape((8, 64, LANES), bf16)
    send = call(
        send_first, buffer(16, 8, 1024),
        [
            pltpu.VMEM((512, LANES), bf16),
            pltpu.VMEM((8, 512), bf16),
            pltpu.VMEM((576, LANES), f32),
            pltpu.SemaphoreType.DMA((2,)),
        ],
        0, 400_000,
        *(pltpu.with_memory_space_constraint(x, pltpu.HBM) for x in (cotangent.reshape(512, LANES), strided_weight)),
        space=pltpu.HBM,
    )
    got = lax.all_to_all(send, "space", 0, 0, tiled=True, axis_index_groups=[ORDER_IN])
    cells_in, _ = lax.optimization_barrier((volume, send))
    across_vol, inside_vol = call(
        split_columns, (plane, plane),
        [pltpu.VMEM((2, 528, LANES), f32), pltpu.VMEM((2, 8, 64, LANES), bf16)], 4_000_000_000, 2_000_000,
        cells_in.reshape(512, 256),
    )
    across_got = lax.ppermute(across_vol, "space", between_chips)
    inside_got = lax.ppermute(inside_vol, "space", in_chip)
    grad_plane = shape((8, LANES, LANES), bf16)
    taps = pltpu.VMEM((3, 10, LANES, LANES), bf16)
    blocks = pltpu.VMEM((256, 512), bf16)
    conv_part = (LANES, 9 * LANES)
    inside_grad, *terms = call(
        inside,
        (
            grad_plane, shape(conv_part, f32), shape((LANES, 512), f32), shape((LANES, 256), f32),
            shape((256, 512), f32), shape((4, LANES, 256), f32),
        ),
        [taps, pltpu.VMEM((256, 512), f32), blocks], 3_000_000_000, 2_000_000,
        across_vol, inside_vol, inside_got, got, conv_weight,
    )
    send, across_grad = call(
        across, (buffer(16, 24, 512), grad_plane),
        [taps, blocks, pltpu.VMEM(conv_part, f32)], 3_000_000_000, 3_000_000,
        across_got, across_vol, inside_vol, got, conv_weight, *terms,
    )
    got = lax.all_to_all(send, "space", 0, 0, tiled=True, axis_index_groups=[ORDER_SLABS])
    own_terms, across_terms, inside_terms = call(
        back, (shape((2, 8, 64, LANES), f32), plane, plane),
        [pltpu.VMEM((2, 10, 256, LANES), bf16), pltpu.VMEM((2, 8, 64, LANES), bf16)],
        3_000_000_000, 3_000_000,
        across_grad, inside_grad, conv_weight,
    )
    got, own_terms, across_terms, inside_terms = lax.optimization_barrier(
        (got, own_terms, across_terms, inside_terms)
    )
    across_got = lax.ppermute(across_terms, "space", between_chips)
    inside_got = lax.ppermute(inside_terms, "space", in_chip)
    send = call(sum_space, buffer(16, 16, 512), [], 0, 600_000, got)
    got_out = got
    got = lax.all_to_all(send, "dp", 0, 0, tiled=True, axis_index_groups=[ORDER_SAMPLES])
    send = call(
        functools.partial(sum_conv, 1.0 / math.sqrt(cells)), buffer(16, 8, 512), [], 0, 300_000, got,
    )
    sums = got
    got = lax.all_to_all(send, "space", 0, 0, tiled=True, axis_index_groups=[ORDER_OUT])
    output, strided_grad, vol_grad = call(
        functools.partial(finish, 1.0 / math.sqrt(cells / 8)),
        (shape((512, LANES), bf16), shape((8, 512), f32), shape((512, 256), bf16)),
        [
            pltpu.VMEM((576, LANES), f32),
            pltpu.VMEM((2, 8, 64, LANES), f32),
            pltpu.VMEM((512, 256), bf16),
            pltpu.VMEM((2, 528, LANES), f32),
        ],
        1_000_000_000, 2_000_000,
        got_out, sums, own_terms, across_got, inside_got,
    )
    conv_grad = call(place_conv, shape((64, 864), f32), [], 0, 300_000, got)
    return output.reshape(cotangent.shape), vol_grad.reshape(volume.shape), conv_grad, strided_grad


def solution(mesh):
    return jax.shard_map(
        shards,
        mesh=mesh,
        in_specs=(
            P("dp", None, "space", None, None),
            P(),
            P("space", None),
            P("dp", "space", None, None, None),
        ),
        out_specs=(
            P("dp", "space", None, None, None),
            P("dp", None, "space", None, None),
            P(),
            P("space", None),
        ),
        check_vma=False,
    )
```
